256 devices in a mesh: group: 4 (over y), block: 64 (over x, z, core).
Axes of the slice: x: 4, y: 4, z: 8, core: 2. Of those that a mesh axis runs over, the one named last changes fastest.
Arguments:
- estimate: float32 [3072, 64, 128], P('block'), may hold values from 0.5 to 2
- recorded: float32 [4, 64, 3072, 128], P('group', 'block'), may hold values from 0.2 to 3
- psf_x: float32 [4, 31], P('group'), may hold values from 0.05 to 1
- psf_y: float32 [4, 31], P('group'), may hold values from 0.05 to 1
- psf_z: float32 [4, 61], P('group'), may hold values from 0.05 to 1
- view_shifts: int32 [4], P('group'), may hold values from -8 to 8, as said below
- view_boxes: int32 [4, 2], P('group'), may hold values from 0 to 3072, as said below
Outputs:
- updated: float32 [3072, 64, 128], P('block')
The draws below stay inside these ranges and needn't reach their ends.
Inputs may be any that keep to these rules, and one draw needn't show every extreme that they name: `view_shifts`: some view has shift 8 and some view has shift -8. `view_boxes`: each view's first cell lies in 0 to 768 and its end in 2304 to 3072; view 0 covers the whole grid.
All inputs are finite; a program needn't handle non-finite values.
Results may differ from the reference program's by a relative error of at most 0.0003.
Values sent between devices are 32-bit elements; how exact they have to be, the bound alone decides.
No kernel may reach another device: no remote copies, remote signals or barrier semaphores. Data moves between devices by JAX's collectives and lax.ppermute only.
A program may use at most 64 MiB of HBM per device.

```python
import math
import jax
import jax.numpy as jnp
from jax import lax

NY = 64
NZ = 128
PSFX = 31
PSFY = 31
PSFZ = 61
SMAX = 8
VIEWS = 4
NX = 3072


def draw_view_shifts(key, part):
    key = jax.random.fold_in(key, 11)
    value_key, offset_key, order_key = jax.random.split(key, 3)
    values = jax.random.randint(value_key, (VIEWS,), -SMAX, SMAX + 1)
    offset = jax.random.randint(offset_key, (), 1, 2 * SMAX + 1)
    moved = (values[2] + SMAX + offset) % (2 * SMAX + 1) - SMAX
    values = values.at[0].set(SMAX).at[1].set(-SMAX).at[3].set(moved)
    order = jax.random.permutation(order_key, VIEWS)
    return values[order].astype(jnp.int32)


def draw_view_boxes(key, part):
    key = jax.random.fold_in(key, 23)
    first_key, second_key = jax.random.split(key)
    starts = jax.random.randint(first_key, (VIEWS,), 0, NX // 4 + 1)
    finish = jax.random.randint(second_key, (VIEWS,), NX - NX // 4, NX + 1)
    starts = starts.at[0].set(0)
    finish = finish.at[0].set(NX)
    return jnp.stack([starts, finish], axis=1).astype(jnp.int32)


def level_of(key, dims, pieces, low, top_value):
    def one(position, parts):
        steps = jax.random.uniform(jax.random.fold_in(jax.random.fold_in(key, 6), position), (parts,), jnp.float32, low / len(pieces), top_value / len(pieces))
        return jnp.repeat(jnp.exp(steps), dims[position] // parts).reshape((-1,) + (1,) * (len(dims) - position - 1))

    loudness = one(*pieces[0])
    for cut in pieces[1:]:
        loudness = loudness * one(*cut)
    return loudness


def setup_inputs(seed: int = 0) -> dict:
    keys = jax.random.split(jax.random.key(seed), 8)
    return {
        "estimate": jnp.clip(jnp.exp(math.log(2.0) - 1.3862944 * jax.random.uniform(keys[0], (NX, NY, NZ), jnp.float32) ** level_of(keys[0], (NX, NY, NZ), ((0, 64),), -0.2, 0.2)), 0.5, 2.0),
        "recorded": jnp.clip(jnp.exp(math.log(3.0) - 2.7080502 * jax.random.uniform(keys[1], (VIEWS, NY, NX, NZ), jnp.float32) ** level_of(keys[1], (VIEWS, NY, NX, NZ), ((0, 4), (1, 64)), -0.2, 0.2)), 0.2, 3.0),
        "psf_x": jnp.clip(jnp.exp(math.log(1.0) - 2.9957323 * jax.random.uniform(keys[2], (VIEWS, PSFX), jnp.float32) ** level_of(keys[2], (VIEWS, PSFX), ((0, 4),), -0.2, 0.2)), 0.05, 1.0),
        "psf_y": jnp.clip(jnp.exp(math.log(1.0) - 2.9957323 * jax.random.uniform(keys[3], (VIEWS, PSFY), jnp.float32) ** level_of(keys[3], (VIEWS, PSFY), ((0, 4),), -0.2, 0.2)), 0.05, 1.0),
        "psf_z": jnp.clip(jnp.exp(math.log(1.0) - 2.9957323 * jax.random.uniform(keys[4], (VIEWS, PSFZ), jnp.float32) ** level_of(keys[4], (VIEWS, PSFZ), ((0, 4),), -0.2, 0.2)), 0.05, 1.0),
        "view_shifts": draw_view_shifts(jax.random.fold_in(keys[7], 71), 0),
        "view_boxes": draw_view_boxes(jax.random.fold_in(keys[7], 71), 0),
    }


def band_matrix(kernel_taps, length):
    half_width = kernel_taps.shape[0] // 2
    row_ids = jnp.arange(length)[:, None]
    col_ids = jnp.arange(length)[None, :]
    tap_index = col_ids - row_ids + half_width
    in_range = (tap_index >= 0) & (tap_index < kernel_taps.shape[0])
    return jnp.where(in_range, kernel_taps[jnp.clip(tap_index, 0, kernel_taps.shape[0] - 1)], jnp.float32(0.0))


def blur_plane(volume, band_y, band_z):
    partial_value = jnp.einsum('xbz,yb->xyz', volume, band_y, precision=lax.Precision.HIGHEST)
    return jnp.einsum('xyz,wz->xyw', partial_value, band_z, precision=lax.Precision.HIGHEST)


def along_x(volume, taps_x, start_base, padding):
    padded = jnp.pad(volume, ((padding, padding), (0, 0), (0, 0)))
    accumulated = jnp.zeros(volume.shape, jnp.float32)
    for tap in range(taps_x.shape[0]):
        start = (start_base(tap) + padding).astype(jnp.int32)
        accumulated = accumulated + taps_x[tap] * lax.dynamic_slice_in_dim(padded, start, volume.shape[0], 0)
    return accumulated


def reference(estimate, recorded, psf_x, psf_y, psf_z, view_shifts, view_boxes):
    half_x = PSFX // 2
    padding = half_x + SMAX
    positions = jnp.arange(NX)
    summed = jnp.zeros(estimate.shape, jnp.float32)
    for index_view in range(VIEWS):
        taps_x = psf_x[index_view] / jnp.sum(psf_x[index_view])
        taps_y = psf_y[index_view] / jnp.sum(psf_y[index_view])
        taps_z = psf_z[index_view] / jnp.sum(psf_z[index_view])
        band_y = band_matrix(taps_y, NY)
        band_z = band_matrix(taps_z, NZ)
        shift_view = view_shifts[index_view]
        blurred = blur_plane(estimate, band_y, band_z)
        predicted = along_x(blurred, taps_x, lambda tap: shift_view + tap - half_x, padding)
        inside = (positions >= view_boxes[index_view, 0]) & (positions < view_boxes[index_view, 1])
        observed = jnp.transpose(recorded[index_view], (1, 0, 2))
        quotient = jnp.where(inside[:, None, None], observed / predicted, jnp.float32(1.0))
        spread = along_x(quotient, taps_x, lambda tap: half_x - shift_view - tap, padding)
        summed = summed + blur_plane(spread, band_y.T, band_z.T)
    return estimate * summed / VIEWS
```

```python
import jax
import jax.numpy as jnp
from jax import lax
from jax.sharding import PartitionSpec as P

PSFX = 31
SMAX = 8


def with_halo(block, axis, width):
    count = lax.axis_size(axis)
    forward = [(i, i + 1) for i in range(count - 1)]
    backward = [(target, source) for source, target in forward]
    low = lax.ppermute(block[block.shape[0] - width :], axis, forward)
    high = lax.ppermute(block[:width], axis, backward)
    return jnp.concatenate([low, block, high], axis=0)


def pick_taps(kernel_taps, tap_index):
    taps = jnp.arange(kernel_taps.shape[0])[:, None, None]
    return jnp.sum(jnp.where(tap_index[None] == taps, kernel_taps[:, None, None], jnp.float32(0.0)), axis=0)


def band_matrix(kernel_taps, length):
    half_width = kernel_taps.shape[0] // 2
    row_ids = jnp.arange(length)[:, None]
    col_ids = jnp.arange(length)[None, :]
    return pick_taps(kernel_taps, col_ids - row_ids + half_width)


def slab_matrix(kernel_taps, slab_rows, wide_rows, forward, offset):
    row_ids = jnp.arange(slab_rows)[:, None]
    col_ids = jnp.arange(wide_rows)[None, :]
    if forward:
        tap_index = col_ids - row_ids - offset
    else:
        tap_index = row_ids - col_ids + offset
    return pick_taps(kernel_taps, tap_index)


def ring_sum(value, axis):
    me = lax.axis_index(axis)
    rows = value.shape[0] // 8
    up = [(i, (i + 1) % 4) for i in range(4)]
    down = [(i, (i + 3) % 4) for i in range(4)]

    def part(step, half):
        start = lax.rem(me + step, 4) * (2 * rows) + half * rows
        return lax.dynamic_slice_in_dim(value, start, rows, 0)

    def send(block, way):
        return lax.ppermute(block, axis, way)

    far_a, far_b = send(part(2, 0), up), send(part(2, 1), down)
    near_b, near_a = send(part(1, 1), up), send(part(3, 0), down)
    sum_a = send(part(1, 0) + far_a, up)
    sum_b = send(part(3, 1) + far_b, down)
    mine_a = part(0, 0) + near_a + sum_a
    mine_b = part(0, 1) + near_b + sum_b
    low_a, high_b = send(mine_a, up), send(mine_b, down)
    low_b, high_a = send(mine_b, up), send(mine_a, down)
    opposite_a, opposite_b = send(low_a, up), send(high_b, down)
    out = jnp.zeros_like(value)
    for step, half, block in (
        (0, 0, mine_a), (0, 1, mine_b), (3, 0, low_a), (3, 1, low_b),
        (1, 0, high_a), (1, 1, high_b), (2, 0, opposite_a), (2, 1, opposite_b),
    ):
        start = lax.rem(me + step, 4) * (2 * rows) + half * rows
        out = lax.dynamic_update_slice_in_dim(out, block, start, 0)
    return out


def blur_plane(volume, band_y, band_z):
    partial_value = jnp.einsum("xbz,yb->xyz", volume, band_y, precision=lax.Precision.HIGHEST)
    return jnp.einsum("xyz,wz->xyw", partial_value, band_z, precision=lax.Precision.HIGHEST)


def body(estimate, recorded, psf_x, psf_y, psf_z, view_shifts, view_boxes):
    slab_rows = estimate.shape[0]
    local_views = recorded.shape[0]
    half_x = PSFX // 2
    margin = half_x + SMAX
    wide_rows = slab_rows + 2 * margin
    first_row = lax.axis_index("block") * slab_rows
    positions = first_row + jnp.arange(slab_rows)
    fetched = lax.all_to_all(recorded, "block", split_axis=2, concat_axis=1, tiled=True)
    taps_x = psf_x[0] / jnp.sum(psf_x[0])
    taps_y = psf_y[0] / jnp.sum(psf_y[0])
    taps_z = psf_z[0] / jnp.sum(psf_z[0])
    band_y = band_matrix(taps_y, estimate.shape[1])
    band_z = band_matrix(taps_z, estimate.shape[2])
    shift_view = view_shifts[0]
    extended = blur_plane(with_halo(estimate, "block", margin), band_y, band_z)
    forward_band = slab_matrix(taps_x, slab_rows, wide_rows, True, shift_view + margin - half_x)
    predicted = jnp.einsum("xe,eyz->xyz", forward_band, extended, precision=lax.Precision.HIGHEST)
    inside = (positions >= view_boxes[0, 0]) & (positions < view_boxes[0, 1])
    observed = jnp.transpose(fetched[0], (1, 0, 2))
    quotient = jnp.where(inside[:, None, None], observed / predicted, jnp.float32(1.0))
    adjoint_part = blur_plane(quotient, band_y.T, band_z.T)
    adjoint_wide = with_halo(adjoint_part, "block", margin)
    backward_band = slab_matrix(taps_x, slab_rows, wide_rows, False, margin + half_x - shift_view)
    summed = jnp.einsum("xe,eyz->xyz", backward_band, adjoint_wide, precision=lax.Precision.HIGHEST)
    combined = ring_sum(summed, "group")
    return estimate * combined / (local_views * lax.axis_size("group"))


def solution(mesh):
    return jax.shard_map(
        body,
        mesh=mesh,
        in_specs=(
            P("block", None, None),
            P("group", "block", None, None),
            P("group", None),
            P("group", None),
            P("group", None),
            P("group"),
            P("group", None),
        ),
        out_specs=P("block", None, None),
        check_vma=False,
    )
```

```python
import functools
import jax
import jax.numpy as jnp
from jax import lax
from jax.experimental import pallas as pl
from jax.experimental.pallas import tpu as pltpu
from jax.sharding import PartitionSpec as P

NX, NY, NZ = 3072, 64, 128
SLAB = 48
HALO = 16
WIDE = SLAB + 2 * HALO
SMAX = 8
TAPS_X, TAPS_Y, TAPS_Z = 31, 31, 61
HALF_X, HALF_Y, HALF_Z = 15, 15, 30
F32, BF16 = jnp.float32, jnp.bfloat16
VMEM_LIMIT = 48 * 1024 * 1024

SMEM_SPEC = pl.BlockSpec(memory_space=pltpu.SMEM)
VMEM_SPEC = pl.BlockSpec(memory_space=pltpu.VMEM)
ANY_SPEC = pl.BlockSpec(memory_space=pl.ANY)
PARAMS = pltpu.CompilerParams(vmem_limit_bytes=VMEM_LIMIT)


def iota(shape, axis):
    return lax.broadcasted_iota(jnp.int32, shape, axis)


def split(value):
    high = value.astype(BF16)
    return high, (value - high.astype(F32)).astype(BF16)


def roll_kernel(shift_ref, source, target, sems):
    shift = shift_ref[0]
    body = NX - 2 * SMAX
    parts = 4
    size = body // parts
    copies = []
    for part in range(parts):
        first = SMAX + part * size
        copies.append(
            pltpu.make_async_copy(
                source.at[pl.ds(first, size)], target.at[pl.ds(first + shift, size)], sems.at[part]
            )
        )
    for edge in range(2 * SMAX):
        row = (NX - SMAX + edge) % NX
        place = lax.rem(row + shift + NX, NX)
        copies.append(
            pltpu.make_async_copy(source.at[pl.ds(row, 1)], target.at[pl.ds(place, 1)], sems.at[parts + edge])
        )
    for copy in copies:
        copy.start()
    for copy in copies:
        copy.wait()


def roll_rows(recorded, shift):
    return pl.pallas_call(
        roll_kernel,
        out_shape=jax.ShapeDtypeStruct((NX, 1, NZ), F32),
        in_specs=[SMEM_SPEC, ANY_SPEC],
        out_specs=ANY_SPEC,
        scratch_shapes=[pltpu.SemaphoreType.DMA((4 + 2 * SMAX,))],
        cost_estimate=pl.CostEstimate(flops=0, bytes_accessed=3 * 2**20, transcendentals=0),
        name="roll_rows",
    )(shift, recorded.reshape(NX, 1, NZ))


def pick_taps(taps_ref, count, tap_index, valid):
    total = taps_ref[0, 0]
    picked = jnp.zeros(tap_index.shape, F32)
    for tap in range(count):
        if tap:
            total = total + taps_ref[0, tap]
        picked = jnp.where(tap_index == tap, taps_ref[0, tap], picked)
    if valid is not None:
        picked = jnp.where(valid, picked, 0.0)
    return picked / jnp.full(tap_index.shape, total, F32)


def packed(matrix, part):
    high, low = split(matrix)
    return jnp.where(part < 2, high.astype(F32), low.astype(F32)).astype(BF16)


def bands_kernel(place_ref, shift_ref, x_ref, y_ref, z_ref, yf_ref, yb_ref, zf_ref, zb_ref, xf_ref, xb_ref):
    shift = shift_ref[0]
    first = place_ref[1] * SLAB
    shape = (NY, 3 * NY)
    row, col = iota(shape, 0), iota(shape, 1)
    part = jnp.where(col >= 2 * NY, 2, jnp.where(col >= NY, 1, 0))
    col = col - part * NY
    yf_ref[...] = packed(pick_taps(y_ref, TAPS_Y, col - row + HALF_Y, None), part)
    yb_ref[...] = packed(pick_taps(y_ref, TAPS_Y, row - col + HALF_Y, None), part)
    shape = (NZ, NZ)
    row, col = iota(shape, 0), iota(shape, 1)
    for ref, index in ((zf_ref, row - col + HALF_Z), (zb_ref, col - row + HALF_Z)):
        high, low = split(pick_taps(z_ref, TAPS_Z, index, None))
        ref[:NZ, :NZ] = high
        ref[NZ:, :NZ] = high
        ref[:NZ, NZ:] = low
        ref[NZ:, NZ:] = jnp.zeros(shape, BF16)
    shape = (SLAB, 3 * WIDE)
    row, col = iota(shape, 0), iota(shape, 1)
    part = jnp.where(col >= 2 * WIDE, 2, jnp.where(col >= WIDE, 1, 0))
    step = col - part * WIDE - HALO - row
    place = first + row
    view_row = place - shift
    view_row = jnp.where(view_row < 0, view_row + NX, view_row)
    view_row = jnp.where(view_row >= NX, view_row - NX, view_row)
    met = view_row + shift + step
    xf_ref[...] = packed(pick_taps(x_ref, TAPS_X, step + HALF_X, (met >= 0) & (met < NX)), part)
    met = place - shift + step
    xb_ref[...] = packed(pick_taps(x_ref, TAPS_X, HALF_X - step, (met >= 0) & (met < NX)), part)


def make_bands(place, shift, psf_x, psf_y, psf_z):
    shapes = [(NY, 3 * NY)] * 2 + [(2 * NZ, 2 * NZ)] * 2 + [(SLAB, 3 * WIDE)] * 2
    return pl.pallas_call(
        bands_kernel,
        out_shape=[jax.ShapeDtypeStruct(shape, BF16) for shape in shapes],
        in_specs=[SMEM_SPEC] * 5,
        out_specs=[VMEM_SPEC] * 6,
        compiler_params=PARAMS,
        name="make_bands",
    )(place, shift, psf_x, psf_y, psf_z)


def blur_z(value, band):
    both = jnp.dot(jnp.concatenate(split(value), axis=1), band, preferred_element_type=F32)
    return both[:, :NZ] + both[:, NZ:]


def blur_rows(band, left, right):
    high, low = split(jnp.concatenate([left, right], axis=1))
    both = jnp.dot(band, jnp.concatenate([high, low, high], axis=0), preferred_element_type=F32)
    return both[:, :NZ], both[:, NZ:]


def forward_kernel(low_ref, own_ref, high_ref, yf_ref, zf_ref, xf_ref, out_ref, blurred, wide):
    for ref, count, base in ((low_ref, HALO, 0), (own_ref, SLAB, HALO), (high_ref, HALO, HALO + SLAB)):

        def along_z(block, carry, ref=ref, base=base):
            rows = ref[pl.ds(block * 8, 8)].reshape(8 * NY, NZ)
            start = pl.multiple_of((base + block * 8) * NY, 8)
            blurred[pl.ds(start, 8 * NY), :] = blur_z(rows, zf_ref[...])
            return carry

        lax.fori_loop(0, count // 8, along_z, 0)

    def along_y(pair, carry):
        start = pl.multiple_of(pair * 2 * NY, 2 * NY)
        left, right = blur_rows(yf_ref[...], blurred[pl.ds(start, NY), :], blurred[pl.ds(start + NY, NY), :])
        wide[pl.ds(start, NY), :] = left
        wide[pl.ds(start + NY, NY), :] = right
        return carry

    lax.fori_loop(0, WIDE // 2, along_y, 0, unroll=4)

    def along_x(pair, carry):
        y = pair * 2
        left, right = blur_rows(
            xf_ref[...], wide[pl.ds(y, WIDE, stride=NY), :], wide[pl.ds(y + 1, WIDE, stride=NY), :]
        )
        out_ref[y] = left
        out_ref[y + 1] = right
        return carry

    lax.fori_loop(0, NY // 2, along_x, 0, unroll=4)


def forward(low, own, high, band_y, band_z, band_x):
    return pl.pallas_call(
        forward_kernel,
        out_shape=jax.ShapeDtypeStruct((NY, SLAB, NZ), F32),
        in_specs=[VMEM_SPEC] * 6,
        out_specs=VMEM_SPEC,
        scratch_shapes=[pltpu.VMEM((WIDE * NY, NZ), F32), pltpu.VMEM((WIDE * NY, NZ), F32)],
        compiler_params=PARAMS,
        cost_estimate=pl.CostEstimate(flops=10**9, bytes_accessed=6 * 2**20, transcendentals=0),
        name="forward",
    )(low, own, high, band_y, band_z, band_x)


def quotient_kernel(chunks, place_ref, shift_ref, box_ref, seen_ref, predicted_ref, yb_ref, zb_ref, *rest):
    out_refs, blurred = rest[:-1], rest[-1]
    step = pl.program_id(0)
    chunk = chunks[0] + step * ((chunks[-1] - chunks[0]) // max(len(chunks) - 1, 1))
    row = place_ref[1] * SLAB + chunk * HALO - shift_ref[0] + iota((HALO, NZ), 0)
    row = jnp.where(row < 0, row + NX, row)
    row = jnp.where(row >= NX, row - NX, row)
    inside = (row >= box_ref[0, 0]) & (row < box_ref[0, 1])

    def along_z(block, carry):
        span = pl.ds(block * 16, 16)
        ratio = jnp.where(inside[None], seen_ref[span] / predicted_ref[span], 1.0)
        start = pl.multiple_of(block * 16 * HALO, 16 * HALO)
        blurred[pl.ds(start, 16 * HALO), :] = blur_z(ratio.reshape(16 * HALO, NZ), zb_ref[...])
        return carry

    lax.fori_loop(0, NY // 16, along_z, 0, unroll=2)

    for index in range(len(chunks)):

        @pl.when(step == index)
        def _(out_ref=out_refs[index]):
            for x in range(0, HALO, 2):
                left, right = blur_rows(
                    yb_ref[...],
                    blurred[pl.ds(x, NY, stride=HALO), :],
                    blurred[pl.ds(x + 1, NY, stride=HALO), :],
                )
                out_ref[x] = left
                out_ref[x + 1] = right


def quotient(chunks, place, shift, box, seen, predicted, band_y, band_z):
    count = len(chunks)
    gap = (chunks[-1] - chunks[0]) // max(count - 1, 1)
    piece = pl.BlockSpec((NY, HALO, NZ), lambda step: (0, chunks[0] + step * gap, 0))
    return pl.pallas_call(
        functools.partial(quotient_kernel, chunks),
        grid=(count,),
        out_shape=[jax.ShapeDtypeStruct((HALO, NY, NZ), F32)] * count,
        in_specs=[SMEM_SPEC] * 3 + [piece, piece] + [VMEM_SPEC] * 2,
        out_specs=[VMEM_SPEC] * count,
        scratch_shapes=[pltpu.VMEM((NY * HALO, NZ), F32)],
        compiler_params=PARAMS,
        cost_estimate=pl.CostEstimate(flops=10**8 * count, bytes_accessed=2**20 * count, transcendentals=0),
        name="quotient",
    )(place, shift, box, seen, predicted, band_y, band_z)


def backward_kernel(parts, place_ref, *rest):
    wide_refs, xb_ref, out_refs = rest[:5], rest[5], rest[6:]
    for out_ref, (turn, half) in zip(out_refs, parts):
        base = lax.rem(place_ref[0] + turn, 4) * 16 + half * 8
        for y in range(0, 8, 2):
            planes = [
                jnp.concatenate([ref[pl.ds(base + y + side, HALO, stride=NY), :] for ref in wide_refs], axis=0)
                for side in (0, 1)
            ]
            left, right = blur_rows(xb_ref[...], *planes)
            out_ref[y] = left
            out_ref[y + 1] = right


def backward(parts, place, wide, band_x):
    return pl.pallas_call(
        functools.partial(backward_kernel, parts),
        out_shape=[jax.ShapeDtypeStruct((8, SLAB, NZ), F32)] * len(parts),
        in_specs=[SMEM_SPEC] + [VMEM_SPEC] * 6,
        out_specs=[VMEM_SPEC] * len(parts),
        compiler_params=PARAMS,
        cost_estimate=pl.CostEstimate(flops=5 * 10**7 * len(parts), bytes_accessed=4 * 2**20, transcendentals=0),
        name="backward",
    )(place, *[piece.reshape(HALO * NY, NZ) for piece in wide], band_x)


def finish_kernel(parts, place_ref, estimate_ref, *rest):
    piece_refs, out_ref = rest[:-1], rest[-1]
    for piece_ref, (turn, half) in zip(piece_refs, parts):
        base = pl.multiple_of(lax.rem(place_ref[0] + turn, 4) * 16 + half * 8, 8)

        def row(x, carry, piece_ref=piece_ref, base=base):
            value = piece_ref[pl.ds(x, 8, stride=SLAB), :]
            out_ref[x, pl.ds(base, 8), :] = estimate_ref[x, pl.ds(base, 8), :] * value * 0.25
            return carry

        lax.fori_loop(0, SLAB, row, 0, unroll=8)


def finish(parts, place, estimate, pieces):
    return pl.pallas_call(
        functools.partial(finish_kernel, parts),
        out_shape=jax.ShapeDtypeStruct((SLAB, NY, NZ), F32),
        in_specs=[SMEM_SPEC] + [VMEM_SPEC] * 9,
        out_specs=VMEM_SPEC,
        compiler_params=PARAMS,
        cost_estimate=pl.CostEstimate(flops=10**6, bytes_accessed=5 * 2**20, transcendentals=0),
        name="finish",
    )(place, estimate, *[piece.reshape(8 * SLAB, NZ) for piece in pieces])


def turn(block, axis, step):
    size = lax.axis_size(axis)
    return lax.ppermute(block, axis, [(i, (i + step) % size) for i in range(size)])


def body(estimate, recorded, psf_x, psf_y, psf_z, view_shifts, view_boxes):
    place = jnp.stack([lax.axis_index("group"), lax.axis_index("block")]).astype(jnp.int32)
    low = turn(estimate[SLAB - HALO :], "block", 1)
    high = turn(estimate[:HALO], "block", -1)
    rolled = roll_rows(recorded, view_shifts).reshape(NY, SLAB, NZ)
    seen = lax.all_to_all(rolled, "block", 0, 0)
    yf, yb, zf, zb, xf, xb = make_bands(place, view_shifts, psf_x, psf_y, psf_z)
    predicted = forward(low, estimate, high, yf, zf, xf)

    args = (place, view_shifts, view_boxes, seen, predicted, yb, zb)
    edge_low, edge_high = quotient((0, 2), *args)
    from_low = turn(edge_high, "block", 1)
    from_high = turn(edge_low, "block", -1)
    (middle,) = quotient((1,), *args)
    wide = (from_low, edge_low, middle, edge_high, from_high)

    far_a, far_b, near_b, near_a = backward(((2, 0), (2, 1), (1, 1), (3, 0)), place, wide, xb)
    far_a, far_b = turn(far_a, "group", 1), turn(far_b, "group", -1)
    near_b, near_a = turn(near_b, "group", 1), turn(near_a, "group", -1)
    next_a, prev_b, own_a, own_b = backward(((1, 0), (3, 1), (0, 0), (0, 1)), place, wide, xb)
    sum_a = turn(next_a + far_a, "group", 1)
    sum_b = turn(prev_b + far_b, "group", -1)
    own_a = own_a + near_a + sum_a
    own_b = own_b + near_b + sum_b
    low_a, high_b = turn(own_a, "group", 1), turn(own_b, "group", -1)
    low_b, high_a = turn(own_b, "group", 1), turn(own_a, "group", -1)
    across_a, across_b = turn(low_a, "group", 1), turn(high_b, "group", -1)
    return finish(
        ((0, 0), (0, 1), (3, 0), (3, 1), (1, 0), (1, 1), (2, 0), (2, 1)),
        place,
        estimate,
        (own_a, own_b, low_a, low_b, high_a, high_b, across_a, across_b),
    )


def solution(mesh):
    return jax.shard_map(
        body,
        mesh=mesh,
        in_specs=(
            P("block", None, None),
            P("group", "block", None, None),
            P("group", None),
            P("group", None),
            P("group", None),
            P("group"),
            P("group", None),
        ),
        out_specs=P("block", None, None),
        check_vma=False,
    )
```

```python
import functools
import jax
import jax.numpy as jnp
from jax import lax
from jax.experimental import pallas as pl
from jax.experimental.pallas import tpu as pltpu
from jax.sharding import PartitionSpec as P

NX, NY, NZ = 3072, 64, 128
SLAB = 48
HALO = 16
WIDE = SLAB + 2 * HALO
SMAX = 8
TAPS_X, TAPS_Y, TAPS_Z = 31, 31, 61
HALF_X, HALF_Y, HALF_Z = 15, 15, 30
F32, BF16 = jnp.float32, jnp.bfloat16
VMEM_LIMIT = 48 * 1024 * 1024

SMEM_SPEC = pl.BlockSpec(memory_space=pltpu.SMEM)
VMEM_SPEC = pl.BlockSpec(memory_space=pltpu.VMEM)
ANY_SPEC = pl.BlockSpec(memory_space=pl.ANY)
PARAMS = pltpu.CompilerParams(vmem_limit_bytes=VMEM_LIMIT)


def iota(shape, axis):
    return lax.broadcasted_iota(jnp.int32, shape, axis)


def split(value):
    high = value.astype(BF16)
    return high, (value - high.astype(F32)).astype(BF16)


def roll_kernel(shift_ref, source, target, padded):
    padded[pl.ds(SMAX, NX), :] = source[...]
    padded[pl.ds(0, SMAX), :] = source[pl.ds(NX - SMAX, SMAX), :]
    padded[pl.ds(SMAX + NX, SMAX), :] = source[pl.ds(0, SMAX), :]
    start = SMAX - shift_ref[0]

    def move(block, carry):
        base = block * 128
        target[pl.ds(pl.multiple_of(base, 128), 128), :] = padded[pl.ds(start + base, 128), :]
        return carry

    lax.fori_loop(0, NX // 128, move, 0)


def roll_rows(recorded, shift):
    return pl.pallas_call(
        roll_kernel,
        out_shape=jax.ShapeDtypeStruct((NX, NZ), F32),
        in_specs=[SMEM_SPEC, VMEM_SPEC],
        out_specs=VMEM_SPEC,
        scratch_shapes=[pltpu.VMEM((NX + 2 * SMAX, NZ), F32)],
        compiler_params=PARAMS,
        cost_estimate=pl.CostEstimate(flops=10**6, bytes_accessed=3 * 2**20, transcendentals=0),
        name="roll_rows",
    )(shift, recorded.reshape(NX, NZ))


def pick_taps(taps_ref, count, tap_index, valid):
    total = taps_ref[0, 0]
    picked = jnp.zeros(tap_index.shape, F32)
    for tap in range(count):
        if tap:
            total = total + taps_ref[0, tap]
        picked = jnp.where(tap_index == tap, taps_ref[0, tap], picked)
    if valid is not None:
        picked = jnp.where(valid, picked, 0.0)
    return picked / jnp.full(tap_index.shape, total, F32)


def packed(matrix, part):
    high, low = split(matrix)
    return jnp.where(part < 2, high.astype(F32), low.astype(F32)).astype(BF16)


def bands_kernel(place_ref, shift_ref, x_ref, y_ref, z_ref, yf_ref, yb_ref, zf_ref, zb_ref, xf_ref, xb_ref):
    shift = shift_ref[0]
    first = place_ref[1] * SLAB
    shape = (NY, 3 * NY)
    row, col = iota(shape, 0), iota(shape, 1)
    part = jnp.where(col >= 2 * NY, 2, jnp.where(col >= NY, 1, 0))
    col = col - part * NY
    yf_ref[...] = packed(pick_taps(y_ref, TAPS_Y, col - row + HALF_Y, None), part)
    yb_ref[...] = packed(pick_taps(y_ref, TAPS_Y, row - col + HALF_Y, None), part)
    shape = (NZ, NZ)
    row, col = iota(shape, 0), iota(shape, 1)
    for ref, index in ((zf_ref, row - col + HALF_Z), (zb_ref, col - row + HALF_Z)):
        high, low = split(pick_taps(z_ref, TAPS_Z, index, None))
        ref[:NZ, :NZ] = high
        ref[NZ:, :NZ] = high
        ref[:NZ, NZ:] = low
        ref[NZ:, NZ:] = jnp.zeros(shape, BF16)
    shape = (SLAB, 3 * WIDE)
    row, col = iota(shape, 0), iota(shape, 1)
    part = jnp.where(col >= 2 * WIDE, 2, jnp.where(col >= WIDE, 1, 0))
    step = col - part * WIDE - HALO - row
    place = first + row
    view_row = place - shift
    view_row = jnp.where(view_row < 0, view_row + NX, view_row)
    view_row = jnp.where(view_row >= NX, view_row - NX, view_row)
    met = view_row + shift + step
    xf_ref[...] = packed(pick_taps(x_ref, TAPS_X, step + HALF_X, (met >= 0) & (met < NX)), part)
    met = place - shift + step
    xb_ref[...] = packed(pick_taps(x_ref, TAPS_X, HALF_X - step, (met >= 0) & (met < NX)), part)


def make_bands(place, shift, psf_x, psf_y, psf_z):
    shapes = [(NY, 3 * NY)] * 2 + [(2 * NZ, 2 * NZ)] * 2 + [(SLAB, 3 * WIDE)] * 2
    return pl.pallas_call(
        bands_kernel,
        out_shape=[jax.ShapeDtypeStruct(shape, BF16) for shape in shapes],
        in_specs=[SMEM_SPEC] * 5,
        out_specs=[VMEM_SPEC] * 6,
        compiler_params=PARAMS,
        name="make_bands",
    )(place, shift, psf_x, psf_y, psf_z)


def blur_z(value, band):
    both = jnp.dot(jnp.concatenate(split(value), axis=1), band, preferred_element_type=F32)
    return both[:, :NZ] + both[:, NZ:]


def blur_rows(band, left, right):
    high, low = split(jnp.concatenate([left, right], axis=1))
    both = jnp.dot(band, jnp.concatenate([high, low, high], axis=0), preferred_element_type=F32)
    return both[:, :NZ], both[:, NZ:]


def forward_kernel(low_ref, own_ref, high_ref, yf_ref, zf_ref, xf_ref, out_ref, blurred, wide):
    for ref, count, base in ((low_ref, HALO, 0), (own_ref, SLAB, HALO), (high_ref, HALO, HALO + SLAB)):

        def along_z(block, carry, ref=ref, base=base):
            rows = ref[pl.ds(block * 8, 8)].reshape(8 * NY, NZ)
            start = pl.multiple_of((base + block * 8) * NY, 8)
            blurred[pl.ds(start, 8 * NY), :] = blur_z(rows, zf_ref[...])
            return carry

        lax.fori_loop(0, count // 8, along_z, 0)

    def along_y(pair, carry):
        start = pl.multiple_of(pair * 2 * NY, 2 * NY)
        left, right = blur_rows(yf_ref[...], blurred[pl.ds(start, NY), :], blurred[pl.ds(start + NY, NY), :])
        wide[pl.ds(start, NY), :] = left
        wide[pl.ds(start + NY, NY), :] = right
        return carry

    lax.fori_loop(0, WIDE // 2, along_y, 0, unroll=4)

    def along_x(pair, carry):
        y = pair * 2
        left, right = blur_rows(
            xf_ref[...], wide[pl.ds(y, WIDE, stride=NY), :], wide[pl.ds(y + 1, WIDE, stride=NY), :]
        )
        out_ref[y] = left
        out_ref[y + 1] = right
        return carry

    lax.fori_loop(0, NY // 2, along_x, 0, unroll=4)


def forward(low, own, high, band_y, band_z, band_x):
    return pl.pallas_call(
        forward_kernel,
        out_shape=jax.ShapeDtypeStruct((NY, SLAB, NZ), F32),
        in_specs=[VMEM_SPEC] * 6,
        out_specs=VMEM_SPEC,
        scratch_shapes=[pltpu.VMEM((WIDE * NY, NZ), F32), pltpu.VMEM((WIDE * NY, NZ), F32)],
        compiler_params=PARAMS,
        cost_estimate=pl.CostEstimate(flops=2 * 10**11, bytes_accessed=6 * 2**20, transcendentals=0),
        name="forward",
    )(low, own, high, band_y, band_z, band_x)


def quotient_kernel(chunks, place_ref, shift_ref, box_ref, seen_ref, predicted_ref, yb_ref, zb_ref, *rest):
    out_refs, blurred = rest[:-1], rest[-1]
    step = pl.program_id(0)
    chunk = chunks[0] + step * ((chunks[-1] - chunks[0]) // max(len(chunks) - 1, 1))
    row = place_ref[1] * SLAB + chunk * HALO - shift_ref[0] + iota((HALO, NZ), 0)
    row = jnp.where(row < 0, row + NX, row)
    row = jnp.where(row >= NX, row - NX, row)
    inside = (row >= box_ref[0, 0]) & (row < box_ref[0, 1])

    def along_z(block, carry):
        span = pl.ds(block * 16, 16)
        ratio = jnp.where(inside[None], seen_ref[span] / predicted_ref[span], 1.0)
        start = pl.multiple_of(block * 16 * HALO, 16 * HALO)
        blurred[pl.ds(start, 16 * HALO), :] = blur_z(ratio.reshape(16 * HALO, NZ), zb_ref[...])
        return carry

    lax.fori_loop(0, NY // 16, along_z, 0, unroll=2)

    for index in range(len(chunks)):

        @pl.when(step == index)
        def _(out_ref=out_refs[index]):
            for x in range(0, HALO, 2):
                left, right = blur_rows(
                    yb_ref[...],
                    blurred[pl.ds(x, NY, stride=HALO), :],
                    blurred[pl.ds(x + 1, NY, stride=HALO), :],
                )
                out_ref[x] = left
                out_ref[x + 1] = right


def quotient(chunks, place, shift, box, seen, predicted, band_y, band_z):
    count = len(chunks)
    gap = (chunks[-1] - chunks[0]) // max(count - 1, 1)
    piece = pl.BlockSpec((NY, HALO, NZ), lambda step: (0, chunks[0] + step * gap, 0))
    return pl.pallas_call(
        functools.partial(quotient_kernel, chunks),
        grid=(count,),
        out_shape=[jax.ShapeDtypeStruct((HALO, NY, NZ), F32)] * count,
        in_specs=[SMEM_SPEC] * 3 + [piece, piece] + [VMEM_SPEC] * 2,
        out_specs=[VMEM_SPEC] * count,
        scratch_shapes=[pltpu.VMEM((NY * HALO, NZ), F32)],
        compiler_params=PARAMS,
        cost_estimate=pl.CostEstimate(flops=10**8 * count, bytes_accessed=2**20 * count, transcendentals=0),
        name="quotient",
    )(place, shift, box, seen, predicted, band_y, band_z)


def backward_kernel(parts, place_ref, *rest):
    wide_refs, xb_ref, out_refs = rest[:5], rest[5], rest[6:]
    for out_ref, (turn, half) in zip(out_refs, parts):
        base = lax.rem(place_ref[0] + turn, 4) * 16 + half * 8
        for y in range(0, 8, 2):
            planes = [
                jnp.concatenate([ref[pl.ds(base + y + side, HALO, stride=NY), :] for ref in wide_refs], axis=0)
                for side in (0, 1)
            ]
            left, right = blur_rows(xb_ref[...], *planes)
            out_ref[y] = left
            out_ref[y + 1] = right


def backward(parts, place, wide, band_x):
    return pl.pallas_call(
        functools.partial(backward_kernel, parts),
        out_shape=[jax.ShapeDtypeStruct((8, SLAB, NZ), F32)] * len(parts),
        in_specs=[SMEM_SPEC] + [VMEM_SPEC] * 6,
        out_specs=[VMEM_SPEC] * len(parts),
        compiler_params=PARAMS,
        cost_estimate=pl.CostEstimate(flops=5 * 10**7 * len(parts), bytes_accessed=4 * 2**20, transcendentals=0),
        name="backward",
    )(place, *[piece.reshape(HALO * NY, NZ) for piece in wide], band_x)


def finish_kernel(parts, place_ref, estimate_ref, *rest):
    piece_refs, out_ref = rest[:-1], rest[-1]
    for piece_ref, (turn, half) in zip(piece_refs, parts):
        base = pl.multiple_of(lax.rem(place_ref[0] + turn, 4) * 16 + half * 8, 8)

        def row(x, carry, piece_ref=piece_ref, base=base):
            value = piece_ref[pl.ds(x, 8, stride=SLAB), :]
            out_ref[x, pl.ds(base, 8), :] = estimate_ref[x, pl.ds(base, 8), :] * value * 0.25
            return carry

        lax.fori_loop(0, SLAB, row, 0, unroll=8)


def finish(parts, place, estimate, pieces):
    return pl.pallas_call(
        functools.partial(finish_kernel, parts),
        out_shape=jax.ShapeDtypeStruct((SLAB, NY, NZ), F32),
        in_specs=[SMEM_SPEC] + [VMEM_SPEC] * 9,
        out_specs=VMEM_SPEC,
        compiler_params=PARAMS,
        cost_estimate=pl.CostEstimate(flops=10**6, bytes_accessed=5 * 2**20, transcendentals=0),
        name="finish",
    )(place, estimate, *[piece.reshape(8 * SLAB, NZ) for piece in pieces])


def turn(block, axis, step):
    size = lax.axis_size(axis)
    return lax.ppermute(block, axis, [(i, (i + step) % size) for i in range(size)])


def body(estimate, recorded, psf_x, psf_y, psf_z, view_shifts, view_boxes):
    place = jnp.stack([lax.axis_index("group"), lax.axis_index("block")]).astype(jnp.int32)
    low = turn(estimate[SLAB - HALO :], "block", 1)
    high = turn(estimate[:HALO], "block", -1)
    rolled = roll_rows(recorded, view_shifts).reshape(NY, SLAB, NZ)
    seen = lax.all_to_all(rolled, "block", 0, 0)
    yf, yb, zf, zb, xf, xb = make_bands(place, view_shifts, psf_x, psf_y, psf_z)
    predicted = forward(low, estimate, high, yf, zf, xf)

    args = (place, view_shifts, view_boxes, seen, predicted, yb, zb)
    edge_low, edge_high = quotient((0, 2), *args)
    from_low = turn(edge_high, "block", 1)
    from_high = turn(edge_low, "block", -1)
    (middle,) = quotient((1,), *args)
    wide = (from_low, edge_low, middle, edge_high, from_high)

    far_a, far_b, near_b, near_a = backward(((2, 0), (2, 1), (1, 1), (3, 0)), place, wide, xb)
    far_a, far_b = turn(far_a, "group", 1), turn(far_b, "group", -1)
    near_b, near_a = turn(near_b, "group", 1), turn(near_a, "group", -1)
    next_a, prev_b, own_a, own_b = backward(((1, 0), (3, 1), (0, 0), (0, 1)), place, wide, xb)
    sum_a = turn(next_a + far_a, "group", 1)
    sum_b = turn(prev_b + far_b, "group", -1)
    own_a = own_a + near_a + sum_a
    own_b = own_b + near_b + sum_b
    low_a, high_b = turn(own_a, "group", 1), turn(own_b, "group", -1)
    low_b, high_a = turn(own_b, "group", 1), turn(own_a, "group", -1)
    across_a, across_b = turn(low_a, "group", 1), turn(high_b, "group", -1)
    return finish(
        ((0, 0), (0, 1), (3, 0), (3, 1), (1, 0), (1, 1), (2, 0), (2, 1)),
        place,
        estimate,
        (own_a, own_b, low_a, low_b, high_a, high_b, across_a, across_b),
    )


def solution(mesh):
    return jax.shard_map(
        body,
        mesh=mesh,
        in_specs=(
            P("block", None, None),
            P("group", "block", None, None),
            P("group", None),
            P("group", None),
            P("group", None),
            P("group"),
            P("group", None),
        ),
        out_specs=P("block", None, None),
        check_vma=False,
    )
```

```python
import functools
import jax
import jax.numpy as jnp
from jax import lax
from jax.experimental import pallas as pl
from jax.experimental.pallas import tpu as pltpu
from jax.sharding import PartitionSpec as P

NX, NY, NZ = 3072, 64, 128
SLAB = 48
HALO = 16
WIDE = SLAB + 2 * HALO
SMAX = 8
QUARTER = NY // 4
TAPS_X, TAPS_Y, TAPS_Z = 31, 31, 61
HALF_X, HALF_Y, HALF_Z = 15, 15, 30
F32, BF16 = jnp.float32, jnp.bfloat16
VMEM_LIMIT = 48 * 1024 * 1024

SHORT = pl.CostEstimate(flops=1000, bytes_accessed=1000, transcendentals=0)
FAR_COST = pl.CostEstimate(flops=2 * 10**9, bytes_accessed=1000, transcendentals=0)
SMEM_SPEC = pl.BlockSpec(memory_space=pltpu.SMEM)
VMEM_SPEC = pl.BlockSpec(memory_space=pltpu.VMEM)
ANY_SPEC = pl.BlockSpec(memory_space=pl.ANY)
PARAMS = pltpu.CompilerParams(vmem_limit_bytes=VMEM_LIMIT)


def iota(shape, axis):
    return lax.broadcasted_iota(jnp.int32, shape, axis)


def split(value):
    high = value.astype(BF16)
    return high, (value - high.astype(F32)).astype(BF16)


def swap(block, over_link):
    size = lax.axis_size("block")
    start = 1 if over_link else 0
    pairs = [(i % size, (i + 1) % size) for i in range(start, size + start, 2)]
    return lax.ppermute(block, "block", pairs + [(target, source) for source, target in pairs])


PARTS = 4


def edges_kernel(block, estimate, far, near, held, in_sems, out_sems):
    odd = lax.rem(block[0], 2)
    half = HALO // 2
    takes, gives = [], []
    for index, (first, out_ref) in enumerate(((odd, far), (1 - odd, near))):
        for part in range(2):
            slot = 2 * index + part
            rows = estimate.at[pl.ds(first * (SLAB - HALO) + part * half, half)]
            takes.append(pltpu.make_async_copy(rows, held.at[slot], in_sems.at[slot]))
            gives.append(
                pltpu.make_async_copy(held.at[slot], out_ref.at[pl.ds(part * half, half)], out_sems.at[slot])
            )
    for copy in takes:
        copy.start()
    for take, give in zip(takes, gives):
        take.wait()
        give.start()
    for give in gives:
        give.wait()


def edges(block, estimate):
    return pl.pallas_call(
        edges_kernel,
        out_shape=[jax.ShapeDtypeStruct((HALO, NY, NZ), F32)] * 2,
        in_specs=[SMEM_SPEC, ANY_SPEC],
        out_specs=[ANY_SPEC] * 2,
        scratch_shapes=[
            pltpu.VMEM((4, HALO // 2, NY, NZ), F32),
            pltpu.SemaphoreType.DMA((4,)),
            pltpu.SemaphoreType.DMA((4,)),
        ],
        compiler_params=pltpu.CompilerParams(vmem_limit_bytes=60 * 1024 * 1024),
        cost_estimate=pl.CostEstimate(flops=1000, bytes_accessed=2**20, transcendentals=0),
        name="edges",
    )(block, estimate)


def roll_kernel(shift_ref, source, target, padded, rolled, sems):
    padded[pl.ds(SMAX, NX), :] = source[...]
    padded[pl.ds(0, SMAX), :] = source[pl.ds(NX - SMAX, SMAX), :]
    padded[pl.ds(SMAX + NX, SMAX), :] = source[pl.ds(0, SMAX), :]
    start = SMAX - shift_ref[0]
    size = NX // PARTS
    copies = []
    for part in range(PARTS):

        def move(block, carry, part=part):
            base = part * size + block * 128
            rolled[pl.ds(pl.multiple_of(base, 128), 128), :] = padded[pl.ds(start + base, 128), :]
            return carry

        lax.fori_loop(0, size // 128, move, 0)
        copy = pltpu.make_async_copy(
            rolled.at[pl.ds(part * size, size)], target.at[pl.ds(part * size, size)], sems.at[part]
        )
        copy.start()
        copies.append(copy)
    for copy in copies:
        copy.wait()


def roll_rows(recorded, shift):
    return pl.pallas_call(
        roll_kernel,
        out_shape=jax.ShapeDtypeStruct((NX, NZ), F32),
        in_specs=[SMEM_SPEC, VMEM_SPEC],
        out_specs=ANY_SPEC,
        scratch_shapes=[
            pltpu.VMEM((NX + 2 * SMAX, NZ), F32),
            pltpu.VMEM((NX, NZ), F32),
            pltpu.SemaphoreType.DMA((PARTS,)),
        ],
        compiler_params=PARAMS,
        cost_estimate=pl.CostEstimate(flops=10**6, bytes_accessed=3 * 2**20, transcendentals=0),
        name="roll_rows",
    )(shift, recorded.reshape(NX, NZ))


def pick_taps(taps_ref, count, tap_index, valid):
    total = taps_ref[0, 0]
    picked = jnp.zeros(tap_index.shape, F32)
    for tap in range(count):
        if tap:
            total = total + taps_ref[0, tap]
        picked = jnp.where(tap_index == tap, taps_ref[0, tap], picked)
    if valid is not None:
        picked = jnp.where(valid, picked, 0.0)
    return picked / jnp.full(tap_index.shape, total, F32)


def packed(matrix, part):
    high, low = split(matrix)
    return jnp.where(part < 2, high.astype(F32), low.astype(F32)).astype(BF16)


def x_places(first, odd, turned):
    shape = (SLAB, 3 * WIDE)
    row, col = iota(shape, 0), iota(shape, 1)
    part = jnp.where(col >= 2 * WIDE, 2, jnp.where(col >= WIDE, 1, 0))
    col = col - part * WIDE
    block = lax.div(col, HALO)
    other = 4 - block if turned else jnp.where((block == 0) | (block == 4), 4 - block, block)
    block_at = jnp.where(odd == 1, other, block)
    return first + row, block_at * HALO + lax.rem(col, HALO) - HALO - row, part


def bands_kernel(group, block, shift_ref, x_ref, y_ref, z_ref, yf_ref, yb_ref, zf_ref, zb_ref, xf_ref, xb_ref):
    shift = shift_ref[0]
    first = block[0] * SLAB
    shape = (NY, 3 * NY)
    row, col = iota(shape, 0), iota(shape, 1)
    part = jnp.where(col >= 2 * NY, 2, jnp.where(col >= NY, 1, 0))
    col = col - part * NY
    yf_ref[...] = packed(pick_taps(y_ref, TAPS_Y, col - row + HALF_Y, None), part)
    row = lax.rem(row + group[0] * QUARTER, NY)
    yb_ref[...] = packed(pick_taps(y_ref, TAPS_Y, row - col + HALF_Y, None), part)
    shape = (NZ, NZ)
    row, col = iota(shape, 0), iota(shape, 1)
    for ref, index in ((zf_ref, row - col + HALF_Z), (zb_ref, col - row + HALF_Z)):
        high, low = split(pick_taps(z_ref, TAPS_Z, index, None))
        ref[:NZ, :NZ] = high
        ref[NZ:, :NZ] = high
        ref[:NZ, NZ:] = low
        ref[NZ:, NZ:] = jnp.zeros(shape, BF16)
    odd = lax.rem(block[0], 2)
    place, step, part = x_places(first, odd, False)
    view_row = place - shift
    view_row = jnp.where(view_row < 0, view_row + NX, view_row)
    view_row = jnp.where(view_row >= NX, view_row - NX, view_row)
    met = view_row + shift + step
    xf_ref[...] = packed(pick_taps(x_ref, TAPS_X, step + HALF_X, (met >= 0) & (met < NX)), part)
    place, step, part = x_places(first, odd, True)
    met = place - shift + step
    xb_ref[...] = packed(pick_taps(x_ref, TAPS_X, HALF_X - step, (met >= 0) & (met < NX)), part)


def make_bands(group, block, shift, psf_x, psf_y, psf_z):
    shapes = [(NY, 3 * NY)] * 2 + [(2 * NZ, 2 * NZ)] * 2 + [(SLAB, 3 * WIDE)] * 2
    return pl.pallas_call(
        bands_kernel,
        out_shape=[jax.ShapeDtypeStruct(shape, BF16) for shape in shapes],
        in_specs=[SMEM_SPEC] * 6,
        out_specs=[VMEM_SPEC] * 6,
        compiler_params=PARAMS,
        name="make_bands",
    )(group, block, shift, psf_x, psf_y, psf_z)


def blur_z(value, band):
    both = jnp.dot(jnp.concatenate(split(value), axis=1), band, preferred_element_type=F32)
    return both[:, :NZ] + both[:, NZ:]


def blur_rows(band, left, right):
    high, low = split(jnp.concatenate([left, right], axis=1))
    both = jnp.dot(band, jnp.concatenate([high, low, high], axis=0), preferred_element_type=F32)
    return both[:, :NZ], both[:, NZ:]


def forward_kernel(far_ref, own_ref, near_ref, yf_ref, zf_ref, xf_ref, out_ref, blurred, wide):
    for ref, count, base in ((far_ref, HALO, 0), (own_ref, SLAB, HALO), (near_ref, HALO, HALO + SLAB)):

        def along_z(block, carry, ref=ref, base=base):
            rows = ref[pl.ds(block * 8, 8)].reshape(8 * NY, NZ)
            start = pl.multiple_of((base + block * 8) * NY, 8)
            blurred[pl.ds(start, 8 * NY), :] = blur_z(rows, zf_ref[...])
            return carry

        lax.fori_loop(0, count // 8, along_z, 0)

    def along_y(pair, carry):
        start = pl.multiple_of(pair * 2 * NY, 2 * NY)
        left, right = blur_rows(yf_ref[...], blurred[pl.ds(start, NY), :], blurred[pl.ds(start + NY, NY), :])
        wide[pl.ds(start, NY), :] = left
        wide[pl.ds(start + NY, NY), :] = right
        return carry

    lax.fori_loop(0, WIDE // 2, along_y, 0, unroll=4)

    def along_x(pair, carry):
        y = pair * 2
        left, right = blur_rows(
            xf_ref[...], wide[pl.ds(y, WIDE, stride=NY), :], wide[pl.ds(y + 1, WIDE, stride=NY), :]
        )
        out_ref[y] = left
        out_ref[y + 1] = right
        return carry

    lax.fori_loop(0, NY // 2, along_x, 0, unroll=4)


def forward(far, own, near, band_y, band_z, band_x):
    return pl.pallas_call(
        forward_kernel,
        out_shape=jax.ShapeDtypeStruct((NY, SLAB, NZ), F32),
        in_specs=[VMEM_SPEC] * 6,
        out_specs=VMEM_SPEC,
        scratch_shapes=[pltpu.VMEM((WIDE * NY, NZ), F32), pltpu.VMEM((WIDE * NY, NZ), F32)],
        compiler_params=PARAMS,
        cost_estimate=pl.CostEstimate(flops=2 * 10**11, bytes_accessed=6 * 2**20, transcendentals=0),
        name="forward",
    )(far, own, near, band_y, band_z, band_x)


def quotient_kernel(block, shift_ref, box_ref, seen_ref, predicted_ref, yb_ref, zb_ref, *rest):
    out_refs, (across_ref, rest_ref), (fetched, blurred, sems) = rest[:3], rest[3:5], rest[5:]
    odd = lax.rem(block[0], 2)
    size = NY // PARTS
    firsts = [pl.multiple_of(first, HALO) for first in (odd * (SLAB - HALO), (1 - odd) * (SLAB - HALO))] + [HALO]
    copies = [
        pltpu.make_async_copy(
            seen_ref.at[pl.ds(part * size, size), pl.ds(first, HALO), :],
            fetched.at[index, pl.ds(part * size, size)],
            sems.at[index, part],
        )
        for index, first in enumerate(firsts)
        for part in range(PARTS)
    ]
    for copy in copies:
        copy.start()
    for copy in copies:
        copy.wait()
    for index, first in enumerate(firsts):
        row = block[0] * SLAB + first - shift_ref[0] + iota((HALO, NZ), 0)
        row = jnp.where(row < 0, row + NX, row)
        row = jnp.where(row >= NX, row - NX, row)
        inside = (row >= box_ref[0, 0]) & (row < box_ref[0, 1])
        for part in range(PARTS):
            span = pl.ds(part * size, size)
            ratio = fetched[index, span] / predicted_ref[span, pl.ds(first, HALO), :]
            ratio = jnp.where(inside[None], ratio, 1.0).reshape(size * HALO, NZ)
            blurred[index, pl.ds(part * size * HALO, size * HALO), :] = blur_z(ratio, zb_ref[...])
        for x in range(0, HALO, 2):
            both = blur_rows(
                yb_ref[...],
                blurred[index, pl.ds(x, NY, stride=HALO), :],
                blurred[index, pl.ds(x + 1, NY, stride=HALO), :],
            )
            for side, plane in enumerate(both):
                out_refs[index][x + side] = plane
                if index == 0:
                    across_ref[x + side] = plane[2 * QUARTER : 3 * QUARTER]
                    rest_ref[x + side, : 2 * QUARTER] = plane[: 2 * QUARTER]
                    rest_ref[x + side, 2 * QUARTER :] = plane[3 * QUARTER :]


def quotient(block, shift, box, seen, predicted, band_y, band_z):
    sizes = (NY, NY, NY, QUARTER, 3 * QUARTER)
    return pl.pallas_call(
        quotient_kernel,
        out_shape=[jax.ShapeDtypeStruct((HALO, size, NZ), F32) for size in sizes],
        in_specs=[SMEM_SPEC] * 3 + [ANY_SPEC] + [VMEM_SPEC] * 3,
        out_specs=[VMEM_SPEC] * len(sizes),
        scratch_shapes=[
            pltpu.VMEM((3, NY, HALO, NZ), F32),
            pltpu.VMEM((3, NY * HALO, NZ), F32),
            pltpu.SemaphoreType.DMA((3, PARTS)),
        ],
        compiler_params=PARAMS,
        cost_estimate=SHORT,
        name="quotient",
    )(block, shift, box, seen, predicted, band_y, band_z)


def backward_kernel(parts, size, piece_ref, *rest):
    whole_refs, band_ref, out_refs = rest[:4], rest[4], rest[5:]
    for out_ref, (at, piece_at) in zip(out_refs, parts):
        for y in range(0, 8, 2):
            planes = [
                jnp.concatenate(
                    [piece_ref[pl.ds(piece_at + y + side, HALO, stride=size), :]]
                    + [ref[pl.ds(at + y + side, HALO, stride=NY), :] for ref in whole_refs],
                    axis=0,
                )
                for side in (0, 1)
            ]
            left, right = blur_rows(band_ref[...], *planes)
            out_ref[y] = left
            out_ref[y + 1] = right


def backward(parts, cost, piece, wholes, band_x):
    size = piece.shape[1]
    return pl.pallas_call(
        functools.partial(backward_kernel, parts, size),
        out_shape=[jax.ShapeDtypeStruct((8, SLAB, NZ), F32)] * len(parts),
        in_specs=[VMEM_SPEC] * 6,
        out_specs=[VMEM_SPEC] * len(parts),
        compiler_params=PARAMS,
        cost_estimate=cost,
        name="backward",
    )(piece.reshape(HALO * size, NZ), *[whole.reshape(HALO * NY, NZ) for whole in wholes], band_x)


def finish_rows(group, estimate_ref, piece_ref, turns, half, out_ref, out_base):
    base = pl.multiple_of(lax.rem(group[0] + turns, 4) * 16 + half * 8, 8)
    at = base if out_base is None else out_base

    def row(x, carry):
        value = piece_ref[pl.ds(x, 8, stride=SLAB), :]
        out_ref[x, pl.ds(at, 8), :] = estimate_ref[x, pl.ds(base, 8), :] * value * 0.25
        return carry

    lax.fori_loop(0, SLAB, row, 0, unroll=8)
    return base


def finish_kernel(parts, group, estimate_ref, *rest):
    piece_refs, out_ref = rest[:-1], rest[-1]
    for piece_ref, (turns, half) in zip(piece_refs, parts):
        finish_rows(group, estimate_ref, piece_ref, turns, half, out_ref, None)


def last_kernel(parts, group, estimate_ref, *rest):
    piece_refs, (_, out_ref, done, sems) = rest[: len(parts)], rest[len(parts) :]
    copies = []
    for index, (piece_ref, (turns, half)) in enumerate(zip(piece_refs, parts)):
        base = finish_rows(group, estimate_ref, piece_ref, turns, half, done, index * 8)
        copy = pltpu.make_async_copy(
            done.at[:, pl.ds(index * 8, 8), :], out_ref.at[:, pl.ds(base, 8), :], sems.at[index]
        )
        copy.start()
        copies.append(copy)
    for copy in copies:
        copy.wait()


def finish(parts, group, estimate, pieces, before=None):
    count = len(parts)
    pieces = [piece.reshape(8 * SLAB, NZ) for piece in pieces]
    shape = jax.ShapeDtypeStruct((SLAB, NY, NZ), F32)
    cost = SHORT
    in_specs = [SMEM_SPEC] + [VMEM_SPEC] * (count + 1)
    if before is None:
        return pl.pallas_call(
            functools.partial(finish_kernel, parts),
            out_shape=shape,
            in_specs=in_specs,
            out_specs=VMEM_SPEC,
            compiler_params=PARAMS,
            cost_estimate=cost,
            name="finish",
        )(group, estimate, *pieces)
    return pl.pallas_call(
        functools.partial(last_kernel, parts),
        out_shape=shape,
        in_specs=in_specs + [ANY_SPEC],
        out_specs=ANY_SPEC,
        scratch_shapes=[pltpu.VMEM((SLAB, 8 * count, NZ), F32), pltpu.SemaphoreType.DMA((count,))],
        input_output_aliases={count + 2: 0},
        compiler_params=PARAMS,
        cost_estimate=cost,
        name="finish_last",
    )(group, estimate, *pieces, before)


def turn(block, axis, step):
    size = lax.axis_size(axis)
    return lax.ppermute(block, axis, [(i, (i + step) % size) for i in range(size)])


def body(estimate, recorded, psf_x, psf_y, psf_z, view_shifts, view_boxes):
    group, block = lax.axis_index("group").reshape(1), lax.axis_index("block").reshape(1)
    far, near = edges(block, estimate)
    far, near = swap(far, True), swap(near, False)
    rolled = roll_rows(recorded, view_shifts)
    seen = lax.all_to_all(rolled.reshape(NY, SLAB, NZ), "block", 0, 0)
    yf, yb, zf, zb, xf, xb = make_bands(group, block, view_shifts, psf_x, psf_y, psf_z)
    predicted = forward(far, estimate, near, yf, zf, xf)

    far, near, middle, across, rest = quotient(block, view_shifts, view_boxes, seen, predicted, yb, zb)
    across, from_near, rest = swap(across, True), swap(near, False), swap(rest, True)
    wholes = (far, middle, near, from_near)

    far_a, far_b = backward(((32, 0), (40, 8)), FAR_COST, across, wholes, xb)
    far_a, far_b = turn(far_a, "group", 1), turn(far_b, "group", -1)
    far_a, far_b = lax.optimization_barrier((far_a, far_b))
    next_a, near_b, near_a, prev_b, own_a, own_b = backward(
        ((16, 16), (24, 24), (48, 32), (56, 40), (0, 0), (8, 8)), SHORT, rest, wholes, xb
    )
    sum_a = turn(next_a + far_a, "group", 1)
    sum_b = turn(prev_b + far_b, "group", -1)
    near_b, near_a = turn(near_b, "group", 1), turn(near_a, "group", -1)
    own_a = own_a + near_a + sum_a
    own_b = own_b + near_b + sum_b

    low_a, high_b = turn(own_a, "group", 1), turn(own_b, "group", -1)
    low_b, high_a = turn(own_b, "group", 1), turn(own_a, "group", -1)
    across_a, across_b = turn(low_a, "group", 1), turn(high_b, "group", -1)
    most = finish(
        ((0, 0), (0, 1), (3, 0), (3, 1), (1, 0), (1, 1)),
        group,
        estimate,
        (own_a, own_b, low_a, low_b, high_a, high_b),
    )
    return finish(((2, 0), (2, 1)), group, estimate, (across_a, across_b), most)


def solution(mesh):
    return jax.shard_map(
        body,
        mesh=mesh,
        in_specs=(
            P("block", None, None),
            P("group", "block", None, None),
            P("group", None),
            P("group", None),
            P("group", None),
            P("group"),
            P("group", None),
        ),
        out_specs=P("block", None, None),
        check_vma=False,
    )
```

```python
import functools
import jax
import jax.numpy as jnp
from jax import lax
from jax.experimental import pallas as pl
from jax.experimental.pallas import tpu as pltpu
from jax.sharding import PartitionSpec as P

NX, NY, NZ = 3072, 64, 128
SLAB = 48
HALO = 16
WIDE = SLAB + 2 * HALO
SMAX = 8
QUARTER = NY // 4
TAPS_X, TAPS_Y, TAPS_Z = 31, 31, 61
HALF_X, HALF_Y, HALF_Z = 15, 15, 30
F32, BF16 = jnp.float32, jnp.bfloat16
VMEM_LIMIT = 48 * 1024 * 1024

SHORT = pl.CostEstimate(flops=1000, bytes_accessed=1000, transcendentals=0)
FAR_COST = pl.CostEstimate(flops=2 * 10**9, bytes_accessed=1000, transcendentals=0)
SMEM_SPEC = pl.BlockSpec(memory_space=pltpu.SMEM)
VMEM_SPEC = pl.BlockSpec(memory_space=pltpu.VMEM)
ANY_SPEC = pl.BlockSpec(memory_space=pl.ANY)
PARAMS = pltpu.CompilerParams(vmem_limit_bytes=VMEM_LIMIT)


def iota(shape, axis):
    return lax.broadcasted_iota(jnp.int32, shape, axis)


def split(value):
    high = value.astype(BF16)
    return high, (value - high.astype(F32)).astype(BF16)


def swap(block, over_link):
    size = lax.axis_size("block")
    start = 1 if over_link else 0
    pairs = [(i % size, (i + 1) % size) for i in range(start, size + start, 2)]
    return lax.ppermute(block, "block", pairs + [(target, source) for source, target in pairs])


PARTS = 4


def depart_kernel(
    block, shift_hbm, source, estimate, target, far, near, shift_ref, padded, rolled, held, in_sems, out_sems, edge_in, edge_out
):
    odd = lax.rem(block[0], 2)
    size, half = NX // PARTS, HALO // 2
    shift_copy = pltpu.make_async_copy(shift_hbm, shift_ref, in_sems.at[PARTS + 2])
    fetches = [
        pltpu.make_async_copy(source.at[pl.ds(NX - SMAX, SMAX)], padded.at[pl.ds(0, SMAX)], in_sems.at[PARTS]),
        pltpu.make_async_copy(source.at[pl.ds(0, SMAX)], padded.at[pl.ds(SMAX + NX, SMAX)], in_sems.at[PARTS + 1]),
    ]
    fetches += [
        pltpu.make_async_copy(
            source.at[pl.ds(part * size, size)], padded.at[pl.ds(SMAX + part * size, size)], in_sems.at[part]
        )
        for part in range(PARTS)
    ]
    takes, gives = [], []
    for index, (first, out_ref) in enumerate(((odd, far), (1 - odd, near))):
        for part in range(2):
            slot = 2 * index + part
            rows = estimate.at[pl.ds(first * (SLAB - HALO) + part * half, half)]
            takes.append(pltpu.make_async_copy(rows, held.at[slot], edge_in.at[slot]))
            gives.append(
                pltpu.make_async_copy(held.at[slot], out_ref.at[pl.ds(part * half, half)], edge_out.at[slot])
            )
    for copy in [shift_copy] + fetches + takes:
        copy.start()
    shift_copy.wait()
    for copy in fetches[:3]:
        copy.wait()
    start = SMAX - shift_ref[0]
    for part in range(PARTS):
        if part + 1 < PARTS:
            fetches[part + 3].wait()

        def move(block, carry, part=part):
            base = part * size + block * 128
            rolled[pl.ds(pl.multiple_of(base, 128), 128), :] = padded[pl.ds(start + base, 128), :]
            return carry

        lax.fori_loop(0, size // 128, move, 0)
        copy = pltpu.make_async_copy(
            rolled.at[pl.ds(part * size, size)], target.at[pl.ds(part * size, size)], out_sems.at[part]
        )
        copy.start()
        gives.append(copy)
    for take, give in zip(takes, gives):
        take.wait()
        give.start()
    for give in gives:
        give.wait()


def depart(block, shift, recorded, estimate):
    edge = jax.ShapeDtypeStruct((HALO, NY, NZ), F32)
    return pl.pallas_call(
        depart_kernel,
        out_shape=[jax.ShapeDtypeStruct((NX, NZ), F32), edge, edge],
        in_specs=[SMEM_SPEC, ANY_SPEC, ANY_SPEC, ANY_SPEC],
        out_specs=[ANY_SPEC] * 3,
        scratch_shapes=[
            pltpu.SMEM((1,), jnp.int32),
            pltpu.VMEM((NX + 2 * SMAX, NZ), F32),
            pltpu.VMEM((NX, NZ), F32),
            pltpu.VMEM((4, HALO // 2, NY, NZ), F32),
            pltpu.SemaphoreType.DMA((PARTS + 3,)),
            pltpu.SemaphoreType.DMA((PARTS,)),
            pltpu.SemaphoreType.DMA((4,)),
            pltpu.SemaphoreType.DMA((4,)),
        ],
        compiler_params=pltpu.CompilerParams(vmem_limit_bytes=60 * 1024 * 1024),
        cost_estimate=pl.CostEstimate(flops=1000, bytes_accessed=2**20, transcendentals=0),
        name="depart",
    )(block, shift, recorded.reshape(NX, NZ), estimate)


def pick_taps(taps_ref, count, tap_index, valid):
    total = taps_ref[0, 0]
    picked = jnp.zeros(tap_index.shape, F32)
    for tap in range(count):
        if tap:
            total = total + taps_ref[0, tap]
        picked = jnp.where(tap_index == tap, taps_ref[0, tap], picked)
    if valid is not None:
        picked = jnp.where(valid, picked, 0.0)
    return picked / jnp.full(tap_index.shape, total, F32)


def packed(matrix, part):
    high, low = split(matrix)
    return jnp.where(part < 2, high.astype(F32), low.astype(F32)).astype(BF16)


def x_places(first, odd, turned):
    shape = (SLAB, 3 * WIDE)
    row, col = iota(shape, 0), iota(shape, 1)
    part = jnp.where(col >= 2 * WIDE, 2, jnp.where(col >= WIDE, 1, 0))
    col = col - part * WIDE
    block = lax.div(col, HALO)
    other = 4 - block if turned else jnp.where((block == 0) | (block == 4), 4 - block, block)
    block_at = jnp.where(odd == 1, other, block)
    return first + row, block_at * HALO + lax.rem(col, HALO) - HALO - row, part


def bands_kernel(group, block, shift_ref, x_ref, y_ref, z_ref, yf_ref, yb_ref, zf_ref, zb_ref, xf_ref, xb_ref):
    shift = shift_ref[0]
    first = block[0] * SLAB
    shape = (NY, 3 * NY)
    row, col = iota(shape, 0), iota(shape, 1)
    part = jnp.where(col >= 2 * NY, 2, jnp.where(col >= NY, 1, 0))
    col = col - part * NY
    yf_ref[...] = packed(pick_taps(y_ref, TAPS_Y, col - row + HALF_Y, None), part)
    row = lax.rem(row + group[0] * QUARTER, NY)
    yb_ref[...] = packed(pick_taps(y_ref, TAPS_Y, row - col + HALF_Y, None), part)
    shape = (NZ, NZ)
    row, col = iota(shape, 0), iota(shape, 1)
    for ref, index in ((zf_ref, row - col + HALF_Z), (zb_ref, col - row + HALF_Z)):
        high, low = split(pick_taps(z_ref, TAPS_Z, index, None))
        ref[:NZ, :NZ] = high
        ref[NZ:, :NZ] = high
        ref[:NZ, NZ:] = low
        ref[NZ:, NZ:] = jnp.zeros(shape, BF16)
    odd = lax.rem(block[0], 2)
    place, step, part = x_places(first, odd, False)
    view_row = place - shift
    view_row = jnp.where(view_row < 0, view_row + NX, view_row)
    view_row = jnp.where(view_row >= NX, view_row - NX, view_row)
    met = view_row + shift + step
    xf_ref[...] = packed(pick_taps(x_ref, TAPS_X, step + HALF_X, (met >= 0) & (met < NX)), part)
    place, step, part = x_places(first, odd, True)
    met = place - shift + step
    xb_ref[...] = packed(pick_taps(x_ref, TAPS_X, HALF_X - step, (met >= 0) & (met < NX)), part)


def make_bands(group, block, shift, psf_x, psf_y, psf_z):
    shapes = [(NY, 3 * NY)] * 2 + [(2 * NZ, 2 * NZ)] * 2 + [(SLAB, 3 * WIDE)] * 2
    return pl.pallas_call(
        bands_kernel,
        out_shape=[jax.ShapeDtypeStruct(shape, BF16) for shape in shapes],
        in_specs=[SMEM_SPEC] * 6,
        out_specs=[VMEM_SPEC] * 6,
        compiler_params=PARAMS,
        name="make_bands",
    )(group, block, shift, psf_x, psf_y, psf_z)


def blur_z(value, band):
    both = jnp.dot(jnp.concatenate(split(value), axis=1), band, preferred_element_type=F32)
    return both[:, :NZ] + both[:, NZ:]


def blur_rows(band, left, right):
    high, low = split(jnp.concatenate([left, right], axis=1))
    both = jnp.dot(band, jnp.concatenate([high, low, high], axis=0), preferred_element_type=F32)
    return both[:, :NZ], both[:, NZ:]


def forward_kernel(far_ref, own_ref, near_ref, yf_ref, zf_ref, xf_ref, out_ref, blurred, wide):
    for ref, count, base in ((far_ref, HALO, 0), (own_ref, SLAB, HALO), (near_ref, HALO, HALO + SLAB)):

        def along_z(block, carry, ref=ref, base=base):
            rows = ref[pl.ds(block * 8, 8)].reshape(8 * NY, NZ)
            start = pl.multiple_of((base + block * 8) * NY, 8)
            blurred[pl.ds(start, 8 * NY), :] = blur_z(rows, zf_ref[...])
            return carry

        lax.fori_loop(0, count // 8, along_z, 0)

    def along_y(pair, carry):
        start = pl.multiple_of(pair * 2 * NY, 2 * NY)
        left, right = blur_rows(yf_ref[...], blurred[pl.ds(start, NY), :], blurred[pl.ds(start + NY, NY), :])
        wide[pl.ds(start, NY), :] = left
        wide[pl.ds(start + NY, NY), :] = right
        return carry

    lax.fori_loop(0, WIDE // 2, along_y, 0, unroll=4)

    def along_x(pair, carry):
        y = pair * 2
        left, right = blur_rows(
            xf_ref[...], wide[pl.ds(y, WIDE, stride=NY), :], wide[pl.ds(y + 1, WIDE, stride=NY), :]
        )
        out_ref[y] = left
        out_ref[y + 1] = right
        return carry

    lax.fori_loop(0, NY // 2, along_x, 0, unroll=4)


def forward(far, own, near, band_y, band_z, band_x):
    return pl.pallas_call(
        forward_kernel,
        out_shape=jax.ShapeDtypeStruct((NY, SLAB, NZ), F32),
        in_specs=[VMEM_SPEC] * 6,
        out_specs=VMEM_SPEC,
        scratch_shapes=[pltpu.VMEM((WIDE * NY, NZ), F32), pltpu.VMEM((WIDE * NY, NZ), F32)],
        compiler_params=PARAMS,
        cost_estimate=pl.CostEstimate(flops=2 * 10**11, bytes_accessed=6 * 2**20, transcendentals=0),
        name="forward",
    )(far, own, near, band_y, band_z, band_x)


def quotient_kernel(block, shift_ref, box_ref, seen_ref, predicted_ref, yb_ref, zb_ref, *rest):
    out_refs, (across_ref, rest_ref), (fetched, blurred, sems) = rest[:3], rest[3:5], rest[5:]
    odd = lax.rem(block[0], 2)
    size = NY // PARTS
    firsts = [pl.multiple_of(first, HALO) for first in (odd * (SLAB - HALO), (1 - odd) * (SLAB - HALO))] + [HALO]
    copies = [
        pltpu.make_async_copy(
            seen_ref.at[pl.ds(part * size, size), pl.ds(first, HALO), :],
            fetched.at[index, pl.ds(part * size, size)],
            sems.at[index, part],
        )
        for index, first in enumerate(firsts)
        for part in range(PARTS)
    ]
    for copy in copies:
        copy.start()
    for index, first in enumerate(firsts):
        for copy in copies[index * PARTS : (index + 1) * PARTS]:
            copy.wait()
        row = block[0] * SLAB + first - shift_ref[0] + iota((HALO, NZ), 0)
        row = jnp.where(row < 0, row + NX, row)
        row = jnp.where(row >= NX, row - NX, row)
        inside = (row >= box_ref[0, 0]) & (row < box_ref[0, 1])
        for part in range(PARTS):
            span = pl.ds(part * size, size)
            ratio = fetched[index, span] / predicted_ref[span, pl.ds(first, HALO), :]
            ratio = jnp.where(inside[None], ratio, 1.0).reshape(size * HALO, NZ)
            blurred[index, pl.ds(part * size * HALO, size * HALO), :] = blur_z(ratio, zb_ref[...])
        for x in range(0, HALO, 2):
            both = blur_rows(
                yb_ref[...],
                blurred[index, pl.ds(x, NY, stride=HALO), :],
                blurred[index, pl.ds(x + 1, NY, stride=HALO), :],
            )
            for side, plane in enumerate(both):
                out_refs[index][x + side] = plane
                if index == 0:
                    across_ref[x + side] = plane[2 * QUARTER : 3 * QUARTER]
                    rest_ref[x + side, : 2 * QUARTER] = plane[: 2 * QUARTER]
                    rest_ref[x + side, 2 * QUARTER :] = plane[3 * QUARTER :]


def quotient(block, shift, box, seen, predicted, band_y, band_z):
    sizes = (NY, NY, NY, QUARTER, 3 * QUARTER)
    return pl.pallas_call(
        quotient_kernel,
        out_shape=[jax.ShapeDtypeStruct((HALO, size, NZ), F32) for size in sizes],
        in_specs=[SMEM_SPEC] * 3 + [ANY_SPEC] + [VMEM_SPEC] * 3,
        out_specs=[VMEM_SPEC] * len(sizes),
        scratch_shapes=[
            pltpu.VMEM((3, NY, HALO, NZ), F32),
            pltpu.VMEM((3, NY * HALO, NZ), F32),
            pltpu.SemaphoreType.DMA((3, PARTS)),
        ],
        compiler_params=PARAMS,
        cost_estimate=SHORT,
        name="quotient",
    )(block, shift, box, seen, predicted, band_y, band_z)


def backward_kernel(parts, size, piece_ref, *rest):
    whole_refs, band_ref, out_refs = rest[:4], rest[4], rest[5:]
    for out_ref, (at, piece_at) in zip(out_refs, parts):
        for y in range(0, 8, 2):
            planes = [
                jnp.concatenate(
                    [piece_ref[pl.ds(piece_at + y + side, HALO, stride=size), :]]
                    + [ref[pl.ds(at + y + side, HALO, stride=NY), :] for ref in whole_refs],
                    axis=0,
                )
                for side in (0, 1)
            ]
            left, right = blur_rows(band_ref[...], *planes)
            out_ref[y] = left
            out_ref[y + 1] = right


def backward(parts, cost, piece, wholes, band_x):
    size = piece.shape[1]
    return pl.pallas_call(
        functools.partial(backward_kernel, parts, size),
        out_shape=[jax.ShapeDtypeStruct((8, SLAB, NZ), F32)] * len(parts),
        in_specs=[VMEM_SPEC] * 6,
        out_specs=[VMEM_SPEC] * len(parts),
        compiler_params=PARAMS,
        cost_estimate=cost,
        name="backward",
    )(piece.reshape(HALO * size, NZ), *[whole.reshape(HALO * NY, NZ) for whole in wholes], band_x)


def finish_rows(group, estimate_ref, piece_ref, turns, half, out_ref, out_base):
    base = pl.multiple_of(lax.rem(group[0] + turns, 4) * 16 + half * 8, 8)
    at = base if out_base is None else out_base

    def row(x, carry):
        value = piece_ref[pl.ds(x, 8, stride=SLAB), :]
        out_ref[x, pl.ds(at, 8), :] = estimate_ref[x, pl.ds(base, 8), :] * value * 0.25
        return carry

    lax.fori_loop(0, SLAB, row, 0, unroll=8)
    return base


def finish_kernel(parts, group, estimate_ref, *rest):
    piece_refs, out_ref = rest[:-1], rest[-1]
    for piece_ref, (turns, half) in zip(piece_refs, parts):
        finish_rows(group, estimate_ref, piece_ref, turns, half, out_ref, None)


def last_kernel(parts, group, estimate_ref, *rest):
    piece_refs, (_, out_ref, done, sems) = rest[: len(parts)], rest[len(parts) :]
    copies = []
    for index, (piece_ref, (turns, half)) in enumerate(zip(piece_refs, parts)):
        base = finish_rows(group, estimate_ref, piece_ref, turns, half, done, index * 8)
        copy = pltpu.make_async_copy(
            done.at[:, pl.ds(index * 8, 8), :], out_ref.at[:, pl.ds(base, 8), :], sems.at[index]
        )
        copy.start()
        copies.append(copy)
    for copy in copies:
        copy.wait()


def finish(parts, group, estimate, pieces, before=None):
    count = len(parts)
    pieces = [piece.reshape(8 * SLAB, NZ) for piece in pieces]
    shape = jax.ShapeDtypeStruct((SLAB, NY, NZ), F32)
    cost = SHORT
    in_specs = [SMEM_SPEC] + [VMEM_SPEC] * (count + 1)
    if before is None:
        return pl.pallas_call(
            functools.partial(finish_kernel, parts),
            out_shape=shape,
            in_specs=in_specs,
            out_specs=VMEM_SPEC,
            compiler_params=PARAMS,
            cost_estimate=cost,
            name="finish",
        )(group, estimate, *pieces)
    return pl.pallas_call(
        functools.partial(last_kernel, parts),
        out_shape=shape,
        in_specs=in_specs + [ANY_SPEC],
        out_specs=ANY_SPEC,
        scratch_shapes=[pltpu.VMEM((SLAB, 8 * count, NZ), F32), pltpu.SemaphoreType.DMA((count,))],
        input_output_aliases={count + 2: 0},
        compiler_params=PARAMS,
        cost_estimate=cost,
        name="finish_last",
    )(group, estimate, *pieces, before)


def turn(block, axis, step):
    size = lax.axis_size(axis)
    return lax.ppermute(block, axis, [(i, (i + step) % size) for i in range(size)])


def body(estimate, recorded, psf_x, psf_y, psf_z, view_shifts, view_boxes):
    group, block = lax.axis_index("group").reshape(1), lax.axis_index("block").reshape(1)
    rolled, far, near = depart(block, view_shifts, recorded, estimate)
    far, near = swap(far, True), swap(near, False)
    seen = lax.all_to_all(rolled.reshape(NY, SLAB, NZ), "block", 0, 0)
    yf, yb, zf, zb, xf, xb = make_bands(group, block, view_shifts, psf_x, psf_y, psf_z)
    predicted = forward(far, estimate, near, yf, zf, xf)

    far, near, middle, across, rest = quotient(block, view_shifts, view_boxes, seen, predicted, yb, zb)
    across, from_near, rest = swap(across, True), swap(near, False), swap(rest, True)
    wholes = (far, middle, near, from_near)

    far_a, far_b = backward(((32, 0), (40, 8)), FAR_COST, across, wholes, xb)
    far_a, far_b = turn(far_a, "group", 1), turn(far_b, "group", -1)
    far_a, far_b = lax.optimization_barrier((far_a, far_b))
    next_a, near_b, near_a, prev_b, own_a, own_b = backward(
        ((16, 16), (24, 24), (48, 32), (56, 40), (0, 0), (8, 8)), SHORT, rest, wholes, xb
    )
    sum_a = turn(next_a + far_a, "group", 1)
    sum_b = turn(prev_b + far_b, "group", -1)
    near_b, near_a = turn(near_b, "group", 1), turn(near_a, "group", -1)
    near_b, near_a = lax.optimization_barrier((near_b, near_a))
    own_a = own_a + near_a + sum_a
    own_b = own_b + near_b + sum_b

    low_a, high_b = turn(own_a, "group", 1), turn(own_b, "group", -1)
    low_b, high_a = turn(own_b, "group", 1), turn(own_a, "group", -1)
    across_a, across_b = turn(low_a, "group", 1), turn(high_b, "group", -1)
    most = finish(
        ((0, 0), (0, 1), (3, 0), (3, 1), (1, 0), (1, 1)),
        group,
        estimate,
        (own_a, own_b, low_a, low_b, high_a, high_b),
    )
    return finish(((2, 0), (2, 1)), group, estimate, (across_a, across_b), most)


def solution(mesh):
    return jax.shard_map(
        body,
        mesh=mesh,
        in_specs=(
            P("block", None, None),
            P("group", "block", None, None),
            P("group", None),
            P("group", None),
            P("group", None),
            P("group"),
            P("group", None),
        ),
        out_specs=P("block", None, None),
        check_vma=False,
    )
```

```python
import functools
import jax
import jax.numpy as jnp
from jax import lax
from jax.experimental import pallas as pl
from jax.experimental.pallas import tpu as pltpu
from jax.sharding import PartitionSpec as P

NX, NY, NZ = 3072, 64, 128
SLAB = 48
HALO = 16
WIDE = SLAB + 2 * HALO
SMAX = 8
QUARTER = NY // 4
TAPS_X, TAPS_Y, TAPS_Z = 31, 31, 61
HALF_X, HALF_Y, HALF_Z = 15, 15, 30
F32, BF16 = jnp.float32, jnp.bfloat16
VMEM_LIMIT = 48 * 1024 * 1024

SHORT = pl.CostEstimate(flops=1000, bytes_accessed=1000, transcendentals=0)
FAR_COST = pl.CostEstimate(flops=2 * 10**9, bytes_accessed=1000, transcendentals=0)
SMEM_SPEC = pl.BlockSpec(memory_space=pltpu.SMEM)
VMEM_SPEC = pl.BlockSpec(memory_space=pltpu.VMEM)
ANY_SPEC = pl.BlockSpec(memory_space=pl.ANY)
PARAMS = pltpu.CompilerParams(vmem_limit_bytes=VMEM_LIMIT)


def iota(shape, axis):
    return lax.broadcasted_iota(jnp.int32, shape, axis)


def split(value):
    high = value.astype(BF16)
    return high, (value - high.astype(F32)).astype(BF16)


def swap(block, over_link):
    size = lax.axis_size("block")
    start = 1 if over_link else 0
    pairs = [(i % size, (i + 1) % size) for i in range(start, size + start, 2)]
    return lax.ppermute(block, "block", pairs + [(target, source) for source, target in pairs])


FETCHES = 2


def depart_kernel(
    block, shift_hbm, source, estimate, target, far, near, shift_ref, padded, rolled, held, shift_sem, in_sem, out_sems, edge_in, edge_out
):
    odd = lax.rem(block[0], 2)
    shift_copy = pltpu.make_async_copy(shift_hbm, shift_ref, shift_sem)
    fetch = pltpu.make_async_copy(source, padded.at[pl.ds(SMAX, NX)], in_sem)
    takes, gives = [], []
    for slot, (first, out_ref) in enumerate(((odd, far), (1 - odd, near))):
        rows = estimate.at[pl.ds(first * (SLAB - HALO), HALO)]
        takes.append(pltpu.make_async_copy(rows, held.at[slot], edge_in.at[slot]))
        gives.append(pltpu.make_async_copy(held.at[slot], out_ref, edge_out.at[slot]))
    for copy in [shift_copy, fetch] + takes:
        copy.start()
    shift_copy.wait()
    fetch.wait()
    padded[pl.ds(0, SMAX), :] = padded[pl.ds(NX, SMAX), :]
    padded[pl.ds(SMAX + NX, SMAX), :] = padded[pl.ds(SMAX, SMAX), :]
    start = SMAX - shift_ref[0]
    size = NX // 2
    for part in range(2):

        def move(index, carry, part=part):
            base = part * size + index * 128
            rolled[pl.ds(pl.multiple_of(base, 128), 128), :] = padded[pl.ds(start + base, 128), :]
            return carry

        lax.fori_loop(0, size // 128, move, 0)
        copy = pltpu.make_async_copy(
            rolled.at[pl.ds(part * size, size)], target.at[pl.ds(part * size, size)], out_sems.at[part]
        )
        copy.start()
        gives.append(copy)
        takes[part].wait()
        gives[part].start()
    for give in gives:
        give.wait()


def depart(block, shift, recorded, estimate):
    edge = jax.ShapeDtypeStruct((HALO, NY, NZ), F32)
    return pl.pallas_call(
        depart_kernel,
        out_shape=[jax.ShapeDtypeStruct((NX, NZ), F32), edge, edge],
        in_specs=[SMEM_SPEC, ANY_SPEC, ANY_SPEC, ANY_SPEC],
        out_specs=[ANY_SPEC] * 3,
        scratch_shapes=[
            pltpu.SMEM((1,), jnp.int32),
            pltpu.VMEM((NX + 2 * SMAX, NZ), F32),
            pltpu.VMEM((NX, NZ), F32),
            pltpu.VMEM((2, HALO, NY, NZ), F32),
            pltpu.SemaphoreType.DMA,
            pltpu.SemaphoreType.DMA,
            pltpu.SemaphoreType.DMA((2,)),
            pltpu.SemaphoreType.DMA((2,)),
            pltpu.SemaphoreType.DMA((2,)),
        ],
        compiler_params=pltpu.CompilerParams(vmem_limit_bytes=60 * 1024 * 1024),
        cost_estimate=pl.CostEstimate(flops=1000, bytes_accessed=2**20, transcendentals=0),
        name="depart",
    )(block, shift, recorded.reshape(NX, NZ), estimate)


def pick_taps(taps_ref, count, tap_index, valid):
    total = taps_ref[0, 0]
    picked = jnp.zeros(tap_index.shape, F32)
    for tap in range(count):
        if tap:
            total = total + taps_ref[0, tap]
        picked = jnp.where(tap_index == tap, taps_ref[0, tap], picked)
    if valid is not None:
        picked = jnp.where(valid, picked, 0.0)
    return picked / jnp.full(tap_index.shape, total, F32)


def packed(matrix, part):
    high, low = split(matrix)
    return jnp.where(part < 2, high.astype(F32), low.astype(F32)).astype(BF16)


def x_places(first, odd, turned):
    shape = (SLAB, 3 * WIDE)
    row, col = iota(shape, 0), iota(shape, 1)
    part = jnp.where(col >= 2 * WIDE, 2, jnp.where(col >= WIDE, 1, 0))
    col = col - part * WIDE
    block = lax.div(col, HALO)
    other = 4 - block if turned else jnp.where((block == 0) | (block == 4), 4 - block, block)
    block_at = jnp.where(odd == 1, other, block)
    return first + row, block_at * HALO + lax.rem(col, HALO) - HALO - row, part


def bands_kernel(group, block, shift_ref, x_ref, y_ref, z_ref, yf_ref, yb_ref, zf_ref, zb_ref, xf_ref, xb_ref):
    shift = shift_ref[0]
    first = block[0] * SLAB
    shape = (NY, 3 * NY)
    row, col = iota(shape, 0), iota(shape, 1)
    part = jnp.where(col >= 2 * NY, 2, jnp.where(col >= NY, 1, 0))
    col = col - part * NY
    yf_ref[...] = packed(pick_taps(y_ref, TAPS_Y, col - row + HALF_Y, None), part)
    row = lax.rem(row + group[0] * QUARTER, NY)
    yb_ref[...] = packed(pick_taps(y_ref, TAPS_Y, row - col + HALF_Y, None), part)
    shape = (NZ, NZ)
    row, col = iota(shape, 0), iota(shape, 1)
    for ref, index in ((zf_ref, row - col + HALF_Z), (zb_ref, col - row + HALF_Z)):
        high, low = split(pick_taps(z_ref, TAPS_Z, index, None))
        ref[:NZ, :NZ] = high
        ref[NZ:, :NZ] = high
        ref[:NZ, NZ:] = low
        ref[NZ:, NZ:] = jnp.zeros(shape, BF16)
    odd = lax.rem(block[0], 2)
    place, step, part = x_places(first, odd, False)
    view_row = place - shift
    view_row = jnp.where(view_row < 0, view_row + NX, view_row)
    view_row = jnp.where(view_row >= NX, view_row - NX, view_row)
    met = view_row + shift + step
    xf_ref[...] = packed(pick_taps(x_ref, TAPS_X, step + HALF_X, (met >= 0) & (met < NX)), part)
    place, step, part = x_places(first, odd, True)
    met = place - shift + step
    xb_ref[...] = packed(pick_taps(x_ref, TAPS_X, HALF_X - step, (met >= 0) & (met < NX)), part)


def make_bands(group, block, shift, psf_x, psf_y, psf_z):
    shapes = [(NY, 3 * NY)] * 2 + [(2 * NZ, 2 * NZ)] * 2 + [(SLAB, 3 * WIDE)] * 2
    return pl.pallas_call(
        bands_kernel,
        out_shape=[jax.ShapeDtypeStruct(shape, BF16) for shape in shapes],
        in_specs=[SMEM_SPEC] * 6,
        out_specs=[VMEM_SPEC] * 6,
        compiler_params=PARAMS,
        name="make_bands",
    )(group, block, shift, psf_x, psf_y, psf_z)


def blur_z(value, band):
    both = jnp.dot(jnp.concatenate(split(value), axis=1), band, preferred_element_type=F32)
    return both[:, :NZ] + both[:, NZ:]


def blur_rows(band, left, right):
    high, low = split(jnp.concatenate([left, right], axis=1))
    both = jnp.dot(band, jnp.concatenate([high, low, high], axis=0), preferred_element_type=F32)
    return both[:, :NZ], both[:, NZ:]


def forward_kernel(far_ref, own_ref, near_ref, yf_ref, zf_ref, xf_ref, out_ref, blurred, wide):
    for ref, count, base in ((far_ref, HALO, 0), (own_ref, SLAB, HALO), (near_ref, HALO, HALO + SLAB)):

        def along_z(block, carry, ref=ref, base=base):
            rows = ref[pl.ds(block * 8, 8)].reshape(8 * NY, NZ)
            start = pl.multiple_of((base + block * 8) * NY, 8)
            blurred[pl.ds(start, 8 * NY), :] = blur_z(rows, zf_ref[...])
            return carry

        lax.fori_loop(0, count // 8, along_z, 0)

    def along_y(pair, carry):
        start = pl.multiple_of(pair * 2 * NY, 2 * NY)
        left, right = blur_rows(yf_ref[...], blurred[pl.ds(start, NY), :], blurred[pl.ds(start + NY, NY), :])
        wide[pl.ds(start, NY), :] = left
        wide[pl.ds(start + NY, NY), :] = right
        return carry

    lax.fori_loop(0, WIDE // 2, along_y, 0, unroll=4)

    def along_x(pair, carry):
        y = pair * 2
        left, right = blur_rows(
            xf_ref[...], wide[pl.ds(y, WIDE, stride=NY), :], wide[pl.ds(y + 1, WIDE, stride=NY), :]
        )
        out_ref[y] = left
        out_ref[y + 1] = right
        return carry

    lax.fori_loop(0, NY // 2, along_x, 0, unroll=4)


def forward(far, own, near, band_y, band_z, band_x):
    return pl.pallas_call(
        forward_kernel,
        out_shape=jax.ShapeDtypeStruct((NY, SLAB, NZ), F32),
        in_specs=[VMEM_SPEC] * 6,
        out_specs=VMEM_SPEC,
        scratch_shapes=[pltpu.VMEM((WIDE * NY, NZ), F32), pltpu.VMEM((WIDE * NY, NZ), F32)],
        compiler_params=PARAMS,
        cost_estimate=pl.CostEstimate(flops=2 * 10**11, bytes_accessed=6 * 2**20, transcendentals=0),
        name="forward",
    )(far, own, near, band_y, band_z, band_x)


def quotient_kernel(block, scalars, seen_ref, predicted_ref, yb_ref, zb_ref, *rest):
    out_refs, (across_ref, rest_ref), (fetched, blurred, sems) = rest[:3], rest[3:5], rest[5:]
    odd = lax.rem(block[0], 2)
    size = NY // FETCHES
    copies = [
        pltpu.make_async_copy(
            seen_ref.at[pl.ds(part * size, size)], fetched.at[pl.ds(part * size, size)], sems.at[part]
        )
        for part in range(FETCHES)
    ]
    for copy in copies:
        copy.start()
    row = block[0] * SLAB - scalars[0] + iota((SLAB, NZ), 0)
    row = jnp.where(row < 0, row + NX, row)
    row = jnp.where(row >= NX, row - NX, row)
    inside = (row >= scalars[1]) & (row < scalars[2])
    for part in range(FETCHES):
        copies[part].wait()
        for y in range(part * size, (part + 1) * size, 16):
            span = pl.ds(y, 16)
            ratio = jnp.where(inside[None], fetched[span] / predicted_ref[span], 1.0)
            blurred[pl.ds(y * SLAB, 16 * SLAB), :] = blur_z(ratio.reshape(16 * SLAB, NZ), zb_ref[...])
    for index, first in enumerate((odd * (SLAB - HALO), (1 - odd) * (SLAB - HALO), HALO)):
        for x in range(0, HALO, 2):
            both = blur_rows(
                yb_ref[...],
                blurred[pl.ds(first + x, NY, stride=SLAB), :],
                blurred[pl.ds(first + x + 1, NY, stride=SLAB), :],
            )
            for side, plane in enumerate(both):
                out_refs[index][x + side] = plane
                if index == 0:
                    across_ref[x + side] = plane[2 * QUARTER : 3 * QUARTER]
                    rest_ref[x + side, : 2 * QUARTER] = plane[: 2 * QUARTER]
                    rest_ref[x + side, 2 * QUARTER :] = plane[3 * QUARTER :]


def quotient(block, scalars, seen, predicted, band_y, band_z):
    sizes = (NY, NY, NY, QUARTER, 3 * QUARTER)
    return pl.pallas_call(
        quotient_kernel,
        out_shape=[jax.ShapeDtypeStruct((HALO, size, NZ), F32) for size in sizes],
        in_specs=[SMEM_SPEC] * 2 + [ANY_SPEC] + [VMEM_SPEC] * 3,
        out_specs=[VMEM_SPEC] * len(sizes),
        scratch_shapes=[
            pltpu.VMEM((NY, SLAB, NZ), F32),
            pltpu.VMEM((NY * SLAB, NZ), F32),
            pltpu.SemaphoreType.DMA((FETCHES,)),
        ],
        compiler_params=PARAMS,
        cost_estimate=SHORT,
        name="quotient",
    )(block, scalars, seen, predicted, band_y, band_z)


def backward_kernel(parts, size, piece_ref, *rest):
    whole_refs, band_ref, out_refs = rest[:4], rest[4], rest[5:]
    for out_ref, (at, piece_at) in zip(out_refs, parts):
        for y in range(0, 8, 2):
            planes = [
                jnp.concatenate(
                    [piece_ref[pl.ds(piece_at + y + side, HALO, stride=size), :]]
                    + [ref[pl.ds(at + y + side, HALO, stride=NY), :] for ref in whole_refs],
                    axis=0,
                )
                for side in (0, 1)
            ]
            left, right = blur_rows(band_ref[...], *planes)
            out_ref[y] = left
            out_ref[y + 1] = right


def backward(parts, cost, piece, wholes, band_x):
    size = piece.shape[1]
    return pl.pallas_call(
        functools.partial(backward_kernel, parts, size),
        out_shape=[jax.ShapeDtypeStruct((8, SLAB, NZ), F32)] * len(parts),
        in_specs=[VMEM_SPEC] * 6,
        out_specs=[VMEM_SPEC] * len(parts),
        compiler_params=PARAMS,
        cost_estimate=cost,
        name="backward",
    )(piece.reshape(HALO * size, NZ), *[whole.reshape(HALO * NY, NZ) for whole in wholes], band_x)


def finish_rows(group, estimate_ref, piece_ref, turns, half, out_ref, out_base):
    base = pl.multiple_of(lax.rem(group[0] + turns, 4) * 16 + half * 8, 8)
    at = base if out_base is None else out_base

    def row(x, carry):
        value = piece_ref[pl.ds(x, 8, stride=SLAB), :]
        out_ref[x, pl.ds(at, 8), :] = estimate_ref[x, pl.ds(base, 8), :] * value * 0.25
        return carry

    lax.fori_loop(0, SLAB, row, 0, unroll=8)
    return base


def finish_kernel(parts, group, estimate_ref, *rest):
    piece_refs, out_ref = rest[:-1], rest[-1]
    for piece_ref, (turns, half) in zip(piece_refs, parts):
        finish_rows(group, estimate_ref, piece_ref, turns, half, out_ref, None)


def last_kernel(parts, group, estimate_ref, *rest):
    piece_refs, (_, out_ref, done, sems) = rest[: len(parts)], rest[len(parts) :]
    copies = []
    for index, (piece_ref, (turns, half)) in enumerate(zip(piece_refs, parts)):
        base = finish_rows(group, estimate_ref, piece_ref, turns, half, done, index * 8)
        copy = pltpu.make_async_copy(
            done.at[:, pl.ds(index * 8, 8), :], out_ref.at[:, pl.ds(base, 8), :], sems.at[index]
        )
        copy.start()
        copies.append(copy)
    for copy in copies:
        copy.wait()


def finish(parts, group, estimate, pieces, before=None):
    count = len(parts)
    pieces = [piece.reshape(8 * SLAB, NZ) for piece in pieces]
    shape = jax.ShapeDtypeStruct((SLAB, NY, NZ), F32)
    cost = SHORT
    in_specs = [SMEM_SPEC] + [VMEM_SPEC] * (count + 1)
    if before is None:
        return pl.pallas_call(
            functools.partial(finish_kernel, parts),
            out_shape=shape,
            in_specs=in_specs,
            out_specs=VMEM_SPEC,
            compiler_params=PARAMS,
            cost_estimate=cost,
            name="finish",
        )(group, estimate, *pieces)
    return pl.pallas_call(
        functools.partial(last_kernel, parts),
        out_shape=shape,
        in_specs=in_specs + [ANY_SPEC],
        out_specs=ANY_SPEC,
        scratch_shapes=[pltpu.VMEM((SLAB, 8 * count, NZ), F32), pltpu.SemaphoreType.DMA((count,))],
        input_output_aliases={count + 2: 0},
        compiler_params=PARAMS,
        cost_estimate=cost,
        name="finish_last",
    )(group, estimate, *pieces, before)


def turn(block, axis, step):
    size = lax.axis_size(axis)
    return lax.ppermute(block, axis, [(i, (i + step) % size) for i in range(size)])


def body(estimate, recorded, psf_x, psf_y, psf_z, view_shifts, view_boxes):
    group, block = lax.axis_index("group").reshape(1), lax.axis_index("block").reshape(1)
    rolled, far, near = depart(block, view_shifts, recorded, estimate)
    scalars = jnp.concatenate([view_shifts, view_boxes[0]])
    far, near = swap(far, True), swap(near, False)
    seen = lax.all_to_all(rolled.reshape(NY, SLAB, NZ), "block", 0, 0)
    yf, yb, zf, zb, xf, xb = make_bands(group, block, scalars, psf_x, psf_y, psf_z)
    predicted = forward(far, estimate, near, yf, zf, xf)

    far, near, middle, across, rest = quotient(block, scalars, seen, predicted, yb, zb)
    across, from_near, rest = swap(across, True), swap(near, False), swap(rest, True)
    wholes = (far, middle, near, from_near)

    far_a, far_b = backward(((32, 0), (40, 8)), FAR_COST, across, wholes, xb)
    far_a, far_b = turn(far_a, "group", 1), turn(far_b, "group", -1)
    far_a, far_b = lax.optimization_barrier((far_a, far_b))
    next_a, near_b, near_a, prev_b, own_a, own_b = backward(
        ((16, 16), (24, 24), (48, 32), (56, 40), (0, 0), (8, 8)), SHORT, rest, wholes, xb
    )
    sum_a = turn(next_a + far_a, "group", 1)
    sum_b = turn(prev_b + far_b, "group", -1)
    near_b, near_a = turn(near_b, "group", 1), turn(near_a, "group", -1)
    near_b, near_a = lax.optimization_barrier((near_b, near_a))
    own_a = own_a + near_a + sum_a
    own_b = own_b + near_b + sum_b

    low_a, high_b = turn(own_a, "group", 1), turn(own_b, "group", -1)
    low_b, high_a = turn(own_b, "group", 1), turn(own_a, "group", -1)
    across_a, across_b = turn(low_a, "group", 1), turn(high_b, "group", -1)
    most = finish(
        ((0, 0), (0, 1), (3, 0), (3, 1), (1, 0), (1, 1)),
        group,
        estimate,
        (own_a, own_b, low_a, low_b, high_a, high_b),
    )
    return finish(((2, 0), (2, 1)), group, estimate, (across_a, across_b), most)


def solution(mesh):
    return jax.shard_map(
        body,
        mesh=mesh,
        in_specs=(
            P("block", None, None),
            P("group", "block", None, None),
            P("group", None),
            P("group", None),
            P("group", None),
            P("group"),
            P("group", None),
        ),
        out_specs=P("block", None, None),
        check_vma=False,
    )
```

```python
import functools
import jax
import jax.numpy as jnp
from jax import lax
from jax.experimental import pallas as pl
from jax.experimental.pallas import tpu as pltpu
from jax.sharding import PartitionSpec as P

NX, NY, NZ = 3072, 64, 128
SLAB = 48
HALO = 16
WIDE = SLAB + 2 * HALO
SMAX = 8
QUARTER = NY // 4
TAPS_X, TAPS_Y, TAPS_Z = 31, 31, 61
HALF_X, HALF_Y, HALF_Z = 15, 15, 30
F32, BF16 = jnp.float32, jnp.bfloat16
VMEM_LIMIT = 48 * 1024 * 1024

SHORT = pl.CostEstimate(flops=1000, bytes_accessed=1000, transcendentals=0)
FAR_COST = pl.CostEstimate(flops=2 * 10**9, bytes_accessed=1000, transcendentals=0)
SMEM_SPEC = pl.BlockSpec(memory_space=pltpu.SMEM)
VMEM_SPEC = pl.BlockSpec(memory_space=pltpu.VMEM)
ANY_SPEC = pl.BlockSpec(memory_space=pl.ANY)
PARAMS = pltpu.CompilerParams(vmem_limit_bytes=VMEM_LIMIT)


def iota(shape, axis):
    return lax.broadcasted_iota(jnp.int32, shape, axis)


def split(value):
    high = value.astype(BF16)
    return high, (value - high.astype(F32)).astype(BF16)


def swap(block, over_link):
    size = lax.axis_size("block")
    start = 1 if over_link else 0
    pairs = [(i % size, (i + 1) % size) for i in range(start, size + start, 2)]
    return lax.ppermute(block, "block", pairs + [(target, source) for source, target in pairs])


FETCHES = 2


def depart_kernel(
    block, shift_hbm, source, estimate, target, far, near, shift_ref, padded, rolled, held, shift_sem, in_sems, out_sems, edge_in, edge_out
):
    odd = lax.rem(block[0], 2)
    half = NX // 2
    first = half + 2 * SMAX
    shift_copy = pltpu.make_async_copy(shift_hbm, shift_ref, shift_sem)
    fetches = [
        pltpu.make_async_copy(source.at[pl.ds(0, first)], padded.at[pl.ds(SMAX, first)], in_sems.at[0]),
        pltpu.make_async_copy(source.at[pl.ds(NX - SMAX, SMAX)], padded.at[pl.ds(0, SMAX)], in_sems.at[1]),
        pltpu.make_async_copy(
            source.at[pl.ds(first, NX - first)], padded.at[pl.ds(SMAX + first, NX - first)], in_sems.at[2]
        ),
    ]
    takes, gives = [], []
    for slot, (edge, out_ref) in enumerate(((odd, far), (1 - odd, near))):
        rows = estimate.at[pl.ds(edge * (SLAB - HALO), HALO)]
        takes.append(pltpu.make_async_copy(rows, held.at[slot], edge_in.at[slot]))
        gives.append(pltpu.make_async_copy(held.at[slot], out_ref, edge_out.at[slot]))
    for copy in [shift_copy] + fetches[:2] + takes + fetches[2:]:
        copy.start()
    shift_copy.wait()
    start = SMAX - shift_ref[0]
    for part in range(2):
        if part == 0:
            fetches[0].wait()
            fetches[1].wait()
        else:
            fetches[2].wait()
            padded[pl.ds(SMAX + NX, SMAX), :] = padded[pl.ds(SMAX, SMAX), :]

        def move(index, carry, part=part):
            base = part * half + index * 128
            rolled[pl.ds(pl.multiple_of(base, 128), 128), :] = padded[pl.ds(start + base, 128), :]
            return carry

        lax.fori_loop(0, half // 128, move, 0)
        copy = pltpu.make_async_copy(
            rolled.at[pl.ds(part * half, half)], target.at[pl.ds(part * half, half)], out_sems.at[part]
        )
        copy.start()
        gives.append(copy)
        if part == 0:
            for slot in range(2):
                takes[slot].wait()
                gives[slot].start()
    for give in gives:
        give.wait()


def depart(block, shift, recorded, estimate):
    edge = jax.ShapeDtypeStruct((HALO, NY, NZ), F32)
    return pl.pallas_call(
        depart_kernel,
        out_shape=[jax.ShapeDtypeStruct((NX, NZ), F32), edge, edge],
        in_specs=[SMEM_SPEC, ANY_SPEC, ANY_SPEC, ANY_SPEC],
        out_specs=[ANY_SPEC] * 3,
        scratch_shapes=[
            pltpu.SMEM((1,), jnp.int32),
            pltpu.VMEM((NX + 2 * SMAX, NZ), F32),
            pltpu.VMEM((NX, NZ), F32),
            pltpu.VMEM((2, HALO, NY, NZ), F32),
            pltpu.SemaphoreType.DMA,
            pltpu.SemaphoreType.DMA((3,)),
            pltpu.SemaphoreType.DMA((2,)),
            pltpu.SemaphoreType.DMA((2,)),
            pltpu.SemaphoreType.DMA((2,)),
        ],
        compiler_params=pltpu.CompilerParams(vmem_limit_bytes=60 * 1024 * 1024),
        cost_estimate=pl.CostEstimate(flops=1000, bytes_accessed=2**20, transcendentals=0),
        name="depart",
    )(block, shift, recorded.reshape(NX, NZ), estimate)


def pick_taps(taps_ref, count, tap_index, valid):
    total = taps_ref[0, 0]
    picked = jnp.zeros(tap_index.shape, F32)
    for tap in range(count):
        if tap:
            total = total + taps_ref[0, tap]
        picked = jnp.where(tap_index == tap, taps_ref[0, tap], picked)
    if valid is not None:
        picked = jnp.where(valid, picked, 0.0)
    return picked / jnp.full(tap_index.shape, total, F32)


def packed(matrix, part):
    high, low = split(matrix)
    return jnp.where(part < 2, high.astype(F32), low.astype(F32)).astype(BF16)


def x_places(first, odd, turned):
    shape = (SLAB, 3 * WIDE)
    row, col = iota(shape, 0), iota(shape, 1)
    part = jnp.where(col >= 2 * WIDE, 2, jnp.where(col >= WIDE, 1, 0))
    col = col - part * WIDE
    block = lax.div(col, HALO)
    other = 4 - block if turned else jnp.where((block == 0) | (block == 4), 4 - block, block)
    block_at = jnp.where(odd == 1, other, block)
    return first + row, block_at * HALO + lax.rem(col, HALO) - HALO - row, part


def bands_kernel(group, block, shift_ref, x_ref, y_ref, z_ref, yf_ref, yb_ref, zf_ref, zb_ref, xf_ref, xb_ref):
    shift = shift_ref[0]
    first = block[0] * SLAB
    shape = (NY, 3 * NY)
    row, col = iota(shape, 0), iota(shape, 1)
    part = jnp.where(col >= 2 * NY, 2, jnp.where(col >= NY, 1, 0))
    col = col - part * NY
    yf_ref[...] = packed(pick_taps(y_ref, TAPS_Y, col - row + HALF_Y, None), part)
    row = lax.rem(row + group[0] * QUARTER, NY)
    yb_ref[...] = packed(pick_taps(y_ref, TAPS_Y, row - col + HALF_Y, None), part)
    shape = (NZ, NZ)
    row, col = iota(shape, 0), iota(shape, 1)
    for ref, index in ((zf_ref, row - col + HALF_Z), (zb_ref, col - row + HALF_Z)):
        high, low = split(pick_taps(z_ref, TAPS_Z, index, None))
        ref[:NZ, :NZ] = high
        ref[NZ:, :NZ] = high
        ref[:NZ, NZ:] = low
        ref[NZ:, NZ:] = jnp.zeros(shape, BF16)
    odd = lax.rem(block[0], 2)
    place, step, part = x_places(first, odd, False)
    view_row = place - shift
    view_row = jnp.where(view_row < 0, view_row + NX, view_row)
    view_row = jnp.where(view_row >= NX, view_row - NX, view_row)
    met = view_row + shift + step
    xf_ref[...] = packed(pick_taps(x_ref, TAPS_X, step + HALF_X, (met >= 0) & (met < NX)), part)
    place, step, part = x_places(first, odd, True)
    met = place - shift + step
    xb_ref[...] = packed(pick_taps(x_ref, TAPS_X, HALF_X - step, (met >= 0) & (met < NX)), part)


def make_bands(group, block, shift, psf_x, psf_y, psf_z):
    shapes = [(NY, 3 * NY)] * 2 + [(2 * NZ, 2 * NZ)] * 2 + [(SLAB, 3 * WIDE)] * 2
    return pl.pallas_call(
        bands_kernel,
        out_shape=[jax.ShapeDtypeStruct(shape, BF16) for shape in shapes],
        in_specs=[SMEM_SPEC] * 6,
        out_specs=[VMEM_SPEC] * 6,
        compiler_params=PARAMS,
        name="make_bands",
    )(group, block, shift, psf_x, psf_y, psf_z)


def blur_z(value, band):
    both = jnp.dot(jnp.concatenate(split(value), axis=1), band, preferred_element_type=F32)
    return both[:, :NZ] + both[:, NZ:]


def blur_rows(band, left, right):
    high, low = split(jnp.concatenate([left, right], axis=1))
    both = jnp.dot(band, jnp.concatenate([high, low, high], axis=0), preferred_element_type=F32)
    return both[:, :NZ], both[:, NZ:]


def forward_kernel(far_ref, own_ref, near_ref, yf_ref, zf_ref, xf_ref, out_ref, blurred, wide):
    for ref, count, base in ((far_ref, HALO, 0), (own_ref, SLAB, HALO), (near_ref, HALO, HALO + SLAB)):

        def along_z(block, carry, ref=ref, base=base):
            rows = ref[pl.ds(block * 8, 8)].reshape(8 * NY, NZ)
            start = pl.multiple_of((base + block * 8) * NY, 8)
            blurred[pl.ds(start, 8 * NY), :] = blur_z(rows, zf_ref[...])
            return carry

        lax.fori_loop(0, count // 8, along_z, 0)

    def along_y(pair, carry):
        start = pl.multiple_of(pair * 2 * NY, 2 * NY)
        left, right = blur_rows(yf_ref[...], blurred[pl.ds(start, NY), :], blurred[pl.ds(start + NY, NY), :])
        wide[pl.ds(start, NY), :] = left
        wide[pl.ds(start + NY, NY), :] = right
        return carry

    lax.fori_loop(0, WIDE // 2, along_y, 0, unroll=4)

    def along_x(pair, carry):
        y = pair * 2
        left, right = blur_rows(
            xf_ref[...], wide[pl.ds(y, WIDE, stride=NY), :], wide[pl.ds(y + 1, WIDE, stride=NY), :]
        )
        out_ref[y] = left
        out_ref[y + 1] = right
        return carry

    lax.fori_loop(0, NY // 2, along_x, 0, unroll=4)


def forward(far, own, near, band_y, band_z, band_x):
    return pl.pallas_call(
        forward_kernel,
        out_shape=jax.ShapeDtypeStruct((NY, SLAB, NZ), F32),
        in_specs=[VMEM_SPEC] * 6,
        out_specs=VMEM_SPEC,
        scratch_shapes=[pltpu.VMEM((WIDE * NY, NZ), F32), pltpu.VMEM((WIDE * NY, NZ), F32)],
        compiler_params=PARAMS,
        cost_estimate=pl.CostEstimate(flops=2 * 10**11, bytes_accessed=6 * 2**20, transcendentals=0),
        name="forward",
    )(far, own, near, band_y, band_z, band_x)


def quotient_kernel(block, scalars, seen_ref, predicted_ref, yb_ref, zb_ref, *rest):
    out_refs, (across_ref, rest_ref), (fetched, blurred, sems) = rest[:3], rest[3:5], rest[5:]
    odd = lax.rem(block[0], 2)
    size = NY // FETCHES
    copies = [
        pltpu.make_async_copy(
            seen_ref.at[pl.ds(part * size, size)], fetched.at[pl.ds(part * size, size)], sems.at[part]
        )
        for part in range(FETCHES)
    ]
    for copy in copies:
        copy.start()
    row = block[0] * SLAB - scalars[0] + iota((SLAB, NZ), 0)
    row = jnp.where(row < 0, row + NX, row)
    row = jnp.where(row >= NX, row - NX, row)
    inside = (row >= scalars[1]) & (row < scalars[2])
    for part in range(FETCHES):
        copies[part].wait()
        for y in range(part * size, (part + 1) * size, 16):
            span = pl.ds(y, 16)
            ratio = jnp.where(inside[None], fetched[span] / predicted_ref[span], 1.0)
            blurred[pl.ds(y * SLAB, 16 * SLAB), :] = blur_z(ratio.reshape(16 * SLAB, NZ), zb_ref[...])
    for index, first in enumerate((odd * (SLAB - HALO), (1 - odd) * (SLAB - HALO), HALO)):
        for x in range(0, HALO, 2):
            both = blur_rows(
                yb_ref[...],
                blurred[pl.ds(first + x, NY, stride=SLAB), :],
                blurred[pl.ds(first + x + 1, NY, stride=SLAB), :],
            )
            for side, plane in enumerate(both):
                out_refs[index][x + side] = plane
                if index == 0:
                    across_ref[x + side] = plane[2 * QUARTER : 3 * QUARTER]
                    rest_ref[x + side, : 2 * QUARTER] = plane[: 2 * QUARTER]
                    rest_ref[x + side, 2 * QUARTER :] = plane[3 * QUARTER :]


def quotient(block, scalars, seen, predicted, band_y, band_z):
    sizes = (NY, NY, NY, QUARTER, 3 * QUARTER)
    return pl.pallas_call(
        quotient_kernel,
        out_shape=[jax.ShapeDtypeStruct((HALO, size, NZ), F32) for size in sizes],
        in_specs=[SMEM_SPEC] * 2 + [ANY_SPEC] + [VMEM_SPEC] * 3,
        out_specs=[VMEM_SPEC] * len(sizes),
        scratch_shapes=[
            pltpu.VMEM((NY, SLAB, NZ), F32),
            pltpu.VMEM((NY * SLAB, NZ), F32),
            pltpu.SemaphoreType.DMA((FETCHES,)),
        ],
        compiler_params=PARAMS,
        cost_estimate=SHORT,
        name="quotient",
    )(block, scalars, seen, predicted, band_y, band_z)


def backward_kernel(parts, size, piece_ref, *rest):
    whole_refs, band_ref, out_refs = rest[:4], rest[4], rest[5:]
    for out_ref, (at, piece_at) in zip(out_refs, parts):
        for y in range(0, 8, 2):
            planes = [
                jnp.concatenate(
                    [piece_ref[pl.ds(piece_at + y + side, HALO, stride=size), :]]
                    + [ref[pl.ds(at + y + side, HALO, stride=NY), :] for ref in whole_refs],
                    axis=0,
                )
                for side in (0, 1)
            ]
            left, right = blur_rows(band_ref[...], *planes)
            out_ref[y] = left
            out_ref[y + 1] = right


def backward(parts, cost, piece, wholes, band_x):
    size = piece.shape[1]
    return pl.pallas_call(
        functools.partial(backward_kernel, parts, size),
        out_shape=[jax.ShapeDtypeStruct((8, SLAB, NZ), F32)] * len(parts),
        in_specs=[VMEM_SPEC] * 6,
        out_specs=[VMEM_SPEC] * len(parts),
        compiler_params=PARAMS,
        cost_estimate=cost,
        name="backward",
    )(piece.reshape(HALO * size, NZ), *[whole.reshape(HALO * NY, NZ) for whole in wholes], band_x)


def finish_rows(group, estimate_ref, piece_ref, turns, half, out_ref, out_base):
    base = pl.multiple_of(lax.rem(group[0] + turns, 4) * 16 + half * 8, 8)
    at = base if out_base is None else out_base

    def row(x, carry):
        value = piece_ref[pl.ds(x, 8, stride=SLAB), :]
        out_ref[x, pl.ds(at, 8), :] = estimate_ref[x, pl.ds(base, 8), :] * value * 0.25
        return carry

    lax.fori_loop(0, SLAB, row, 0, unroll=8)
    return base


def finish_kernel(parts, group, estimate_ref, *rest):
    piece_refs, out_ref = rest[:-1], rest[-1]
    for piece_ref, (turns, half) in zip(piece_refs, parts):
        finish_rows(group, estimate_ref, piece_ref, turns, half, out_ref, None)


def last_kernel(parts, group, estimate_ref, *rest):
    piece_refs, (_, out_ref, done, sems) = rest[: len(parts)], rest[len(parts) :]
    copies = []
    for index, (piece_ref, (turns, half)) in enumerate(zip(piece_refs, parts)):
        base = finish_rows(group, estimate_ref, piece_ref, turns, half, done, index * 8)
        copy = pltpu.make_async_copy(
            done.at[:, pl.ds(index * 8, 8), :], out_ref.at[:, pl.ds(base, 8), :], sems.at[index]
        )
        copy.start()
        copies.append(copy)
    for copy in copies:
        copy.wait()


def finish(parts, group, estimate, pieces, before=None):
    count = len(parts)
    pieces = [piece.reshape(8 * SLAB, NZ) for piece in pieces]
    shape = jax.ShapeDtypeStruct((SLAB, NY, NZ), F32)
    cost = SHORT
    in_specs = [SMEM_SPEC] + [VMEM_SPEC] * (count + 1)
    if before is None:
        return pl.pallas_call(
            functools.partial(finish_kernel, parts),
            out_shape=shape,
            in_specs=in_specs,
            out_specs=VMEM_SPEC,
            compiler_params=PARAMS,
            cost_estimate=cost,
            name="finish",
        )(group, estimate, *pieces)
    return pl.pallas_call(
        functools.partial(last_kernel, parts),
        out_shape=shape,
        in_specs=in_specs + [ANY_SPEC],
        out_specs=ANY_SPEC,
        scratch_shapes=[pltpu.VMEM((SLAB, 8 * count, NZ), F32), pltpu.SemaphoreType.DMA((count,))],
        input_output_aliases={count + 2: 0},
        compiler_params=PARAMS,
        cost_estimate=cost,
        name="finish_last",
    )(group, estimate, *pieces, before)


def turn(block, axis, step):
    size = lax.axis_size(axis)
    return lax.ppermute(block, axis, [(i, (i + step) % size) for i in range(size)])


def body(estimate, recorded, psf_x, psf_y, psf_z, view_shifts, view_boxes):
    group, block = lax.axis_index("group").reshape(1), lax.axis_index("block").reshape(1)
    rolled, far, near = depart(block, view_shifts, recorded, estimate)
    scalars = jnp.concatenate([view_shifts, view_boxes[0]])
    far, near = swap(far, True), swap(near, False)
    seen = lax.all_to_all(rolled.reshape(NY, SLAB, NZ), "block", 0, 0)
    yf, yb, zf, zb, xf, xb = make_bands(group, block, scalars, psf_x, psf_y, psf_z)
    predicted = forward(far, estimate, near, yf, zf, xf)

    far, near, middle, across, rest = quotient(block, scalars, seen, predicted, yb, zb)
    across, from_near, rest = swap(across, True), swap(near, False), swap(rest, True)
    wholes = (far, middle, near, from_near)

    far_a, far_b = backward(((32, 0), (40, 8)), FAR_COST, across, wholes, xb)
    far_a, far_b = turn(far_a, "group", 1), turn(far_b, "group", -1)
    far_a, far_b = lax.optimization_barrier((far_a, far_b))
    next_a, near_b, near_a, prev_b, own_a, own_b = backward(
        ((16, 16), (24, 24), (48, 32), (56, 40), (0, 0), (8, 8)), SHORT, rest, wholes, xb
    )
    sum_a = turn(next_a + far_a, "group", 1)
    sum_b = turn(prev_b + far_b, "group", -1)
    near_b, near_a = turn(near_b, "group", 1), turn(near_a, "group", -1)
    near_b, near_a = lax.optimization_barrier((near_b, near_a))
    own_a = own_a + near_a + sum_a
    own_b = own_b + near_b + sum_b

    low_a, high_b = turn(own_a, "group", 1), turn(own_b, "group", -1)
    low_b, high_a = turn(own_b, "group", 1), turn(own_a, "group", -1)
    across_a, across_b = turn(low_a, "group", 1), turn(high_b, "group", -1)
    most = finish(
        ((0, 0), (0, 1), (3, 0), (3, 1), (1, 0), (1, 1)),
        group,
        estimate,
        (own_a, own_b, low_a, low_b, high_a, high_b),
    )
    most = finish(((2, 0),), group, estimate, (across_a,), most)
    return finish(((2, 1),), group, estimate, (across_b,), most)


def solution(mesh):
    return jax.shard_map(
        body,
        mesh=mesh,
        in_specs=(
            P("block", None, None),
            P("group", "block", None, None),
            P("group", None),
            P("group", None),
            P("group", None),
            P("group"),
            P("group", None),
        ),
        out_specs=P("block", None, None),
        check_vma=False,
    )
```

```python
import functools
import jax
import jax.numpy as jnp
from jax import lax
from jax.experimental import pallas as pl
from jax.experimental.pallas import tpu as pltpu
from jax.sharding import PartitionSpec as P

NX, NY, NZ = 3072, 64, 128
SLAB = 48
HALO = 16
WIDE = SLAB + 2 * HALO
SMAX = 8
QUARTER = NY // 4
TAPS_X, TAPS_Y, TAPS_Z = 31, 31, 61
HALF_X, HALF_Y, HALF_Z = 15, 15, 30
F32, BF16 = jnp.float32, jnp.bfloat16
VMEM_LIMIT = 48 * 1024 * 1024

SHORT = pl.CostEstimate(flops=1000, bytes_accessed=1000, transcendentals=0)
FAR_COST = pl.CostEstimate(flops=5 * 10**9, bytes_accessed=1000, transcendentals=0)
SMEM_SPEC = pl.BlockSpec(memory_space=pltpu.SMEM)
VMEM_SPEC = pl.BlockSpec(memory_space=pltpu.VMEM)
ANY_SPEC = pl.BlockSpec(memory_space=pl.ANY)
PARAMS = pltpu.CompilerParams(vmem_limit_bytes=VMEM_LIMIT)


def iota(shape, axis):
    return lax.broadcasted_iota(jnp.int32, shape, axis)


def split(value):
    high = value.astype(BF16)
    return high, (value - high.astype(F32)).astype(BF16)


def swap(block, over_link):
    size = lax.axis_size("block")
    start = 1 if over_link else 0
    pairs = [(i % size, (i + 1) % size) for i in range(start, size + start, 2)]
    return lax.ppermute(block, "block", pairs + [(target, source) for source, target in pairs])


FETCHES = 2


def depart_kernel(
    block, shift_hbm, source, estimate, target, far, near, shift_ref, padded, rolled, held, shift_sem, in_sems, out_sems, edge_in, edge_out
):
    odd = lax.rem(block[0], 2)
    half = NX // 2
    first = half + 2 * SMAX
    shift_copy = pltpu.make_async_copy(shift_hbm, shift_ref, shift_sem)
    fetches = [
        pltpu.make_async_copy(source.at[pl.ds(0, first)], padded.at[pl.ds(SMAX, first)], in_sems.at[0]),
        pltpu.make_async_copy(source.at[pl.ds(NX - SMAX, SMAX)], padded.at[pl.ds(0, SMAX)], in_sems.at[1]),
        pltpu.make_async_copy(
            source.at[pl.ds(first, NX - first)], padded.at[pl.ds(SMAX + first, NX - first)], in_sems.at[2]
        ),
    ]
    takes, gives = [], []
    for slot, (edge, out_ref) in enumerate(((odd, far), (1 - odd, near))):
        rows = estimate.at[pl.ds(edge * (SLAB - HALO), HALO)]
        takes.append(pltpu.make_async_copy(rows, held.at[slot], edge_in.at[slot]))
        gives.append(pltpu.make_async_copy(held.at[slot], out_ref, edge_out.at[slot]))
    for copy in [shift_copy] + fetches[:2] + takes + fetches[2:]:
        copy.start()
    shift_copy.wait()
    start = SMAX - shift_ref[0]
    for part in range(2):
        if part == 0:
            fetches[0].wait()
            fetches[1].wait()
        else:
            fetches[2].wait()
            padded[pl.ds(SMAX + NX, SMAX), :] = padded[pl.ds(SMAX, SMAX), :]

        def move(index, carry, part=part):
            base = part * half + index * 128
            rolled[pl.ds(pl.multiple_of(base, 128), 128), :] = padded[pl.ds(start + base, 128), :]
            return carry

        lax.fori_loop(0, half // 128, move, 0)
        copy = pltpu.make_async_copy(
            rolled.at[pl.ds(part * half, half)], target.at[pl.ds(part * half, half)], out_sems.at[part]
        )
        copy.start()
        gives.append(copy)
        if part == 0:
            for slot in range(2):
                takes[slot].wait()
                gives[slot].start()
    for give in gives:
        give.wait()


def depart(block, shift, recorded, estimate):
    edge = jax.ShapeDtypeStruct((HALO, NY, NZ), F32)
    return pl.pallas_call(
        depart_kernel,
        out_shape=[jax.ShapeDtypeStruct((NX, NZ), F32), edge, edge],
        in_specs=[SMEM_SPEC, ANY_SPEC, ANY_SPEC, ANY_SPEC],
        out_specs=[ANY_SPEC] * 3,
        scratch_shapes=[
            pltpu.SMEM((1,), jnp.int32),
            pltpu.VMEM((NX + 2 * SMAX, NZ), F32),
            pltpu.VMEM((NX, NZ), F32),
            pltpu.VMEM((2, HALO, NY, NZ), F32),
            pltpu.SemaphoreType.DMA,
            pltpu.SemaphoreType.DMA((3,)),
            pltpu.SemaphoreType.DMA((2,)),
            pltpu.SemaphoreType.DMA((2,)),
            pltpu.SemaphoreType.DMA((2,)),
        ],
        compiler_params=pltpu.CompilerParams(vmem_limit_bytes=60 * 1024 * 1024),
        cost_estimate=pl.CostEstimate(flops=1000, bytes_accessed=2**20, transcendentals=0),
        name="depart",
    )(block, shift, recorded.reshape(NX, NZ), estimate)


def pick_taps(taps_ref, count, tap_index, valid):
    total = taps_ref[0, 0]
    picked = jnp.zeros(tap_index.shape, F32)
    for tap in range(count):
        if tap:
            total = total + taps_ref[0, tap]
        picked = jnp.where(tap_index == tap, taps_ref[0, tap], picked)
    if valid is not None:
        picked = jnp.where(valid, picked, 0.0)
    return picked / jnp.full(tap_index.shape, total, F32)


def packed(matrix, part):
    high, low = split(matrix)
    return jnp.where(part < 2, high.astype(F32), low.astype(F32)).astype(BF16)


def x_places(first, odd, turned):
    shape = (SLAB, 3 * WIDE)
    row, col = iota(shape, 0), iota(shape, 1)
    part = jnp.where(col >= 2 * WIDE, 2, jnp.where(col >= WIDE, 1, 0))
    col = col - part * WIDE
    block = lax.div(col, HALO)
    other = 4 - block if turned else jnp.where((block == 0) | (block == 4), 4 - block, block)
    block_at = jnp.where(odd == 1, other, block)
    return first + row, block_at * HALO + lax.rem(col, HALO) - HALO - row, part


def bands_kernel(group, block, shift_ref, x_ref, y_ref, z_ref, yf_ref, yb_ref, zf_ref, zb_ref, xf_ref, xb_ref):
    shift = shift_ref[0]
    first = block[0] * SLAB
    shape = (NY, 3 * NY)
    row, col = iota(shape, 0), iota(shape, 1)
    part = jnp.where(col >= 2 * NY, 2, jnp.where(col >= NY, 1, 0))
    col = col - part * NY
    yf_ref[...] = packed(pick_taps(y_ref, TAPS_Y, col - row + HALF_Y, None), part)
    row = lax.rem(row + group[0] * QUARTER, NY)
    yb_ref[...] = packed(pick_taps(y_ref, TAPS_Y, row - col + HALF_Y, None), part)
    shape = (NZ, NZ)
    row, col = iota(shape, 0), iota(shape, 1)
    for ref, index in ((zf_ref, row - col + HALF_Z), (zb_ref, col - row + HALF_Z)):
        high, low = split(pick_taps(z_ref, TAPS_Z, index, None))
        ref[:NZ, :NZ] = high
        ref[NZ:, :NZ] = high
        ref[:NZ, NZ:] = low
        ref[NZ:, NZ:] = jnp.zeros(shape, BF16)
    odd = lax.rem(block[0], 2)
    place, step, part = x_places(first, odd, False)
    view_row = place - shift
    view_row = jnp.where(view_row < 0, view_row + NX, view_row)
    view_row = jnp.where(view_row >= NX, view_row - NX, view_row)
    met = view_row + shift + step
    xf_ref[...] = packed(pick_taps(x_ref, TAPS_X, step + HALF_X, (met >= 0) & (met < NX)), part)
    place, step, part = x_places(first, odd, True)
    met = place - shift + step
    xb_ref[...] = packed(pick_taps(x_ref, TAPS_X, HALF_X - step, (met >= 0) & (met < NX)), part)


def make_bands(group, block, shift, psf_x, psf_y, psf_z):
    shapes = [(NY, 3 * NY)] * 2 + [(2 * NZ, 2 * NZ)] * 2 + [(SLAB, 3 * WIDE)] * 2
    return pl.pallas_call(
        bands_kernel,
        out_shape=[jax.ShapeDtypeStruct(shape, BF16) for shape in shapes],
        in_specs=[SMEM_SPEC] * 6,
        out_specs=[VMEM_SPEC] * 6,
        compiler_params=PARAMS,
        name="make_bands",
    )(group, block, shift, psf_x, psf_y, psf_z)


def blur_z(value, band):
    both = jnp.dot(jnp.concatenate(split(value), axis=1), band, preferred_element_type=F32)
    return both[:, :NZ] + both[:, NZ:]


def blur_rows(band, left, right):
    high, low = split(jnp.concatenate([left, right], axis=1))
    both = jnp.dot(band, jnp.concatenate([high, low, high], axis=0), preferred_element_type=F32)
    return both[:, :NZ], both[:, NZ:]


def forward_kernel(far_ref, own_ref, near_ref, yf_ref, zf_ref, xf_ref, out_ref, blurred, wide):
    for ref, count, base in ((far_ref, HALO, 0), (own_ref, SLAB, HALO), (near_ref, HALO, HALO + SLAB)):

        def along_z(block, carry, ref=ref, base=base):
            rows = ref[pl.ds(block * 8, 8)].reshape(8 * NY, NZ)
            start = pl.multiple_of((base + block * 8) * NY, 8)
            blurred[pl.ds(start, 8 * NY), :] = blur_z(rows, zf_ref[...])
            return carry

        lax.fori_loop(0, count // 8, along_z, 0)

    def along_y(pair, carry):
        start = pl.multiple_of(pair * 2 * NY, 2 * NY)
        left, right = blur_rows(yf_ref[...], blurred[pl.ds(start, NY), :], blurred[pl.ds(start + NY, NY), :])
        wide[pl.ds(start, NY), :] = left
        wide[pl.ds(start + NY, NY), :] = right
        return carry

    lax.fori_loop(0, WIDE // 2, along_y, 0, unroll=4)

    def along_x(pair, carry):
        y = pair * 2
        left, right = blur_rows(
            xf_ref[...], wide[pl.ds(y, WIDE, stride=NY), :], wide[pl.ds(y + 1, WIDE, stride=NY), :]
        )
        out_ref[y] = left
        out_ref[y + 1] = right
        return carry

    lax.fori_loop(0, NY // 2, along_x, 0, unroll=4)


def forward(far, own, near, band_y, band_z, band_x):
    return pl.pallas_call(
        forward_kernel,
        out_shape=jax.ShapeDtypeStruct((NY, SLAB, NZ), F32),
        in_specs=[VMEM_SPEC] * 6,
        out_specs=VMEM_SPEC,
        scratch_shapes=[pltpu.VMEM((WIDE * NY, NZ), F32), pltpu.VMEM((WIDE * NY, NZ), F32)],
        compiler_params=PARAMS,
        cost_estimate=pl.CostEstimate(flops=2 * 10**11, bytes_accessed=6 * 2**20, transcendentals=0),
        name="forward",
    )(far, own, near, band_y, band_z, band_x)


def store(ref, x, plane, spans):
    at = 0
    for low, high in spans:
        ref[x, at : at + high - low] = plane[low:high]
        at += high - low


WHOLE = ((0, NY),)
FAR_FIRST, FAR_REST = ((32, 56),), ((0, 32), (56, 64))
NEAR_FIRST, NEAR_REST = ((32, 48),), ((0, 32), (48, 64))


def rows_of(spans):
    return sum(high - low for low, high in spans)


SENT = ((0, FAR_FIRST), (0, FAR_REST), (1, NEAR_FIRST), (1, NEAR_REST))


def quotient_kernel(block, scalars, seen_ref, predicted_ref, yb_ref, zb_ref, *rest):
    out_refs, piece_refs, (fetched, blurred, sems) = rest[:3], rest[3:-3], rest[-3:]
    odd = lax.rem(block[0], 2)
    size = NY // FETCHES
    copies = [
        pltpu.make_async_copy(
            seen_ref.at[pl.ds(part * size, size)], fetched.at[pl.ds(part * size, size)], sems.at[part]
        )
        for part in range(FETCHES)
    ]
    for copy in copies:
        copy.start()
    row = block[0] * SLAB - scalars[0] + iota((SLAB, NZ), 0)
    row = jnp.where(row < 0, row + NX, row)
    row = jnp.where(row >= NX, row - NX, row)
    inside = (row >= scalars[1]) & (row < scalars[2])
    for part in range(FETCHES):
        copies[part].wait()
        for y in range(part * size, (part + 1) * size, 16):
            span = pl.ds(y, 16)
            ratio = jnp.where(inside[None], fetched[span] / predicted_ref[span], 1.0)
            blurred[pl.ds(y * SLAB, 16 * SLAB), :] = blur_z(ratio.reshape(16 * SLAB, NZ), zb_ref[...])
    for index, first in enumerate((odd * (SLAB - HALO), (1 - odd) * (SLAB - HALO), HALO)):
        for x in range(0, HALO, 2):
            both = blur_rows(
                yb_ref[...],
                blurred[pl.ds(first + x, NY, stride=SLAB), :],
                blurred[pl.ds(first + x + 1, NY, stride=SLAB), :],
            )
            for side, plane in enumerate(both):
                out_refs[index][x + side] = plane
                for ref, (of, spans) in zip(piece_refs, SENT):
                    if of == index:
                        store(ref, x + side, plane, spans)


def quotient(block, scalars, seen, predicted, band_y, band_z):
    sizes = [NY] * 3 + [rows_of(spans) for _, spans in SENT]
    return pl.pallas_call(
        quotient_kernel,
        out_shape=[jax.ShapeDtypeStruct((HALO, size, NZ), F32) for size in sizes],
        in_specs=[SMEM_SPEC] * 2 + [ANY_SPEC] + [VMEM_SPEC] * 3,
        out_specs=[VMEM_SPEC] * len(sizes),
        scratch_shapes=[
            pltpu.VMEM((NY, SLAB, NZ), F32),
            pltpu.VMEM((NY * SLAB, NZ), F32),
            pltpu.SemaphoreType.DMA((FETCHES,)),
        ],
        compiler_params=PARAMS,
        cost_estimate=SHORT,
        name="quotient",
    )(block, scalars, seen, predicted, band_y, band_z)


def find(spans, row):
    at = 0
    for low, high in spans:
        if low <= row < high:
            return at + row - low
        at += high - low
    return None


def backward_kernel(starts, spans, *refs):
    count = len(spans)
    received, own, band_ref, out_refs = refs[:count], refs[count : count + 3], refs[count + 3], refs[count + 4 :]

    def rows(ref, size, at):
        return ref[pl.ds(at, HALO, stride=size), :]

    def arrived(side, row):
        for ref, (of, piece) in zip(received, spans):
            at = find(piece, row) if of == side else None
            if at is not None:
                return rows(ref, rows_of(piece), at)
        raise ValueError(row)

    for out_ref, start in zip(out_refs, starts):
        for y in range(start, start + 8, 2):
            planes = [
                jnp.concatenate(
                    [arrived("far", row)] + [rows(ref, NY, row) for ref in own] + [arrived("near", row)], axis=0
                )
                for row in (y, y + 1)
            ]
            left, right = blur_rows(band_ref[...], *planes)
            out_ref[y - start] = left
            out_ref[y - start + 1] = right


def backward(starts, cost, received, own, band_x):
    spans = tuple((side, piece) for side, piece, _ in received)
    flat = [value.reshape(-1, NZ) for _, _, value in received] + [value.reshape(-1, NZ) for value in own]
    return pl.pallas_call(
        functools.partial(backward_kernel, starts, spans),
        out_shape=[jax.ShapeDtypeStruct((8, SLAB, NZ), F32)] * len(starts),
        in_specs=[VMEM_SPEC] * (len(flat) + 1),
        out_specs=[VMEM_SPEC] * len(starts),
        compiler_params=PARAMS,
        cost_estimate=cost,
        name="backward",
    )(*flat, band_x)


def finish_rows(group, estimate_ref, piece_ref, turns, half, out_ref, out_base):
    base = pl.multiple_of(lax.rem(group[0] + turns, 4) * 16 + half * 8, 8)
    at = base if out_base is None else out_base

    def row(x, carry):
        value = piece_ref[pl.ds(x, 8, stride=SLAB), :]
        out_ref[x, pl.ds(at, 8), :] = estimate_ref[x, pl.ds(base, 8), :] * value * 0.25
        return carry

    lax.fori_loop(0, SLAB, row, 0, unroll=8)
    return base


def finish_kernel(parts, group, estimate_ref, *rest):
    piece_refs, out_ref = rest[:-1], rest[-1]
    for piece_ref, (turns, half) in zip(piece_refs, parts):
        finish_rows(group, estimate_ref, piece_ref, turns, half, out_ref, None)


def last_kernel(parts, group, estimate_ref, *rest):
    piece_refs, (_, out_ref, done, sems) = rest[: len(parts)], rest[len(parts) :]
    copies = []
    for index, (piece_ref, (turns, half)) in enumerate(zip(piece_refs, parts)):
        base = finish_rows(group, estimate_ref, piece_ref, turns, half, done, index * 8)
        copy = pltpu.make_async_copy(
            done.at[:, pl.ds(index * 8, 8), :], out_ref.at[:, pl.ds(base, 8), :], sems.at[index]
        )
        copy.start()
        copies.append(copy)
    for copy in copies:
        copy.wait()


def finish(parts, group, estimate, pieces, before=None):
    count = len(parts)
    pieces = [piece.reshape(8 * SLAB, NZ) for piece in pieces]
    shape = jax.ShapeDtypeStruct((SLAB, NY, NZ), F32)
    cost = SHORT
    in_specs = [SMEM_SPEC] + [VMEM_SPEC] * (count + 1)
    if before is None:
        return pl.pallas_call(
            functools.partial(finish_kernel, parts),
            out_shape=shape,
            in_specs=in_specs,
            out_specs=VMEM_SPEC,
            compiler_params=PARAMS,
            cost_estimate=cost,
            name="finish",
        )(group, estimate, *pieces)
    return pl.pallas_call(
        functools.partial(last_kernel, parts),
        out_shape=shape,
        in_specs=in_specs + [ANY_SPEC],
        out_specs=ANY_SPEC,
        scratch_shapes=[pltpu.VMEM((SLAB, 8 * count, NZ), F32), pltpu.SemaphoreType.DMA((count,))],
        input_output_aliases={count + 2: 0},
        compiler_params=PARAMS,
        cost_estimate=cost,
        name="finish_last",
    )(group, estimate, *pieces, before)


def turn(block, axis, step):
    size = lax.axis_size(axis)
    return lax.ppermute(block, axis, [(i, (i + step) % size) for i in range(size)])


def body(estimate, recorded, psf_x, psf_y, psf_z, view_shifts, view_boxes):
    group, block = lax.axis_index("group").reshape(1), lax.axis_index("block").reshape(1)
    rolled, far, near = depart(block, view_shifts, recorded, estimate)
    scalars = jnp.concatenate([view_shifts, view_boxes[0]])
    far, near = swap(far, True), swap(near, False)
    seen = lax.all_to_all(rolled.reshape(NY, SLAB, NZ), "block", 0, 0)
    yf, yb, zf, zb, xf, xb = make_bands(group, block, scalars, psf_x, psf_y, psf_z)
    predicted = forward(far, estimate, near, yf, zf, xf)

    far, near, middle, far_first, far_rest, near_first, near_rest = quotient(block, scalars, seen, predicted, yb, zb)
    far_first = ("far", FAR_FIRST, swap(far_first, True))
    far_rest = ("far", FAR_REST, swap(far_rest, True))
    near_first = ("near", NEAR_FIRST, swap(near_first, False))
    near_rest = ("near", NEAR_REST, swap(near_rest, False))
    slab = (far, middle, near)

    far_a, far_b = backward((32, 40), FAR_COST, (far_first, near_first), slab, xb)
    far_a, far_b = turn(far_a, "group", 1), turn(far_b, "group", -1)
    next_a, near_b, near_a, prev_b, own_a, own_b = backward(
        (16, 24, 48, 56, 0, 8), SHORT, (far_first, far_rest, near_rest), slab, xb
    )
    sum_a = turn(next_a + far_a, "group", 1)
    sum_b = turn(prev_b + far_b, "group", -1)
    near_b, near_a = turn(near_b, "group", 1), turn(near_a, "group", -1)
    near_b, near_a = lax.optimization_barrier((near_b, near_a))
    own_a = own_a + near_a + sum_a
    own_b = own_b + near_b + sum_b

    low_a, high_b = turn(own_a, "group", 1), turn(own_b, "group", -1)
    low_b, high_a = turn(own_b, "group", 1), turn(own_a, "group", -1)
    across_a, across_b = turn(low_a, "group", 1), turn(high_b, "group", -1)
    most = finish(
        ((0, 0), (0, 1), (3, 0), (3, 1), (1, 0), (1, 1)),
        group,
        estimate,
        (own_a, own_b, low_a, low_b, high_a, high_b),
    )
    most = finish(((2, 0),), group, estimate, (across_a,), most)
    return finish(((2, 1),), group, estimate, (across_b,), most)


def solution(mesh):
    return jax.shard_map(
        body,
        mesh=mesh,
        in_specs=(
            P("block", None, None),
            P("group", "block", None, None),
            P("group", None),
            P("group", None),
            P("group", None),
            P("group"),
            P("group", None),
        ),
        out_specs=P("block", None, None),
        check_vma=False,
    )
```

```python
import functools
import jax
import jax.numpy as jnp
from jax import lax
from jax.experimental import pallas as pl
from jax.experimental.pallas import tpu as pltpu
from jax.sharding import PartitionSpec as P

NX, NY, NZ = 3072, 64, 128
SLAB = 48
HALO = 16
WIDE = SLAB + 2 * HALO
SMAX = 8
QUARTER = NY // 4
TAPS_X, TAPS_Y, TAPS_Z = 31, 31, 61
HALF_X, HALF_Y, HALF_Z = 15, 15, 30
F32, BF16 = jnp.float32, jnp.bfloat16
VMEM_LIMIT = 48 * 1024 * 1024

SHORT = pl.CostEstimate(flops=1000, bytes_accessed=1000, transcendentals=0)
FAR_COST = pl.CostEstimate(flops=2 * 10**9, bytes_accessed=1000, transcendentals=0)
SMEM_SPEC = pl.BlockSpec(memory_space=pltpu.SMEM)
VMEM_SPEC = pl.BlockSpec(memory_space=pltpu.VMEM)
ANY_SPEC = pl.BlockSpec(memory_space=pl.ANY)
PARAMS = pltpu.CompilerParams(vmem_limit_bytes=VMEM_LIMIT)


def iota(shape, axis):
    return lax.broadcasted_iota(jnp.int32, shape, axis)


def split(value):
    high = value.astype(BF16)
    return high, (value - high.astype(F32)).astype(BF16)


def swap(block, over_link):
    size = lax.axis_size("block")
    start = 1 if over_link else 0
    pairs = [(i % size, (i + 1) % size) for i in range(start, size + start, 2)]
    return lax.ppermute(block, "block", pairs + [(target, source) for source, target in pairs])


FETCHES = 2


def depart_kernel(
    block, shift_hbm, source, estimate, target, far, near, shift_ref, padded, rolled, held, shift_sem, in_sems, out_sems, edge_in, edge_out
):
    odd = lax.rem(block[0], 2)
    half = NX // 2
    first = half + 2 * SMAX
    shift_copy = pltpu.make_async_copy(shift_hbm, shift_ref, shift_sem)
    fetches = [
        pltpu.make_async_copy(source.at[pl.ds(0, first)], padded.at[pl.ds(SMAX, first)], in_sems.at[0]),
        pltpu.make_async_copy(source.at[pl.ds(NX - SMAX, SMAX)], padded.at[pl.ds(0, SMAX)], in_sems.at[1]),
        pltpu.make_async_copy(
            source.at[pl.ds(first, NX - first)], padded.at[pl.ds(SMAX + first, NX - first)], in_sems.at[2]
        ),
    ]
    takes, gives = [], []
    for slot, (edge, out_ref) in enumerate(((odd, far), (1 - odd, near))):
        rows = estimate.at[pl.ds(edge * (SLAB - HALO), HALO)]
        takes.append(pltpu.make_async_copy(rows, held.at[slot], edge_in.at[slot]))
        gives.append(pltpu.make_async_copy(held.at[slot], out_ref, edge_out.at[slot]))
    for copy in [shift_copy] + fetches[:2] + takes + fetches[2:]:
        copy.start()
    shift_copy.wait()
    start = SMAX - shift_ref[0]
    for part in range(2):
        if part == 0:
            fetches[0].wait()
            fetches[1].wait()
        else:
            fetches[2].wait()
            padded[pl.ds(SMAX + NX, SMAX), :] = padded[pl.ds(SMAX, SMAX), :]

        def move(index, carry, part=part):
            base = part * half + index * 128
            rolled[pl.ds(pl.multiple_of(base, 128), 128), :] = padded[pl.ds(start + base, 128), :]
            return carry

        lax.fori_loop(0, half // 128, move, 0)
        copy = pltpu.make_async_copy(
            rolled.at[pl.ds(part * half, half)], target.at[pl.ds(part * half, half)], out_sems.at[part]
        )
        copy.start()
        gives.append(copy)
        if part == 0:
            for slot in range(2):
                takes[slot].wait()
                gives[slot].start()
    for give in gives:
        give.wait()


def depart(block, shift, recorded, estimate):
    edge = jax.ShapeDtypeStruct((HALO, NY, NZ), F32)
    return pl.pallas_call(
        depart_kernel,
        out_shape=[jax.ShapeDtypeStruct((NX, NZ), F32), edge, edge],
        in_specs=[SMEM_SPEC, ANY_SPEC, ANY_SPEC, ANY_SPEC],
        out_specs=[ANY_SPEC] * 3,
        scratch_shapes=[
            pltpu.SMEM((1,), jnp.int32),
            pltpu.VMEM((NX + 2 * SMAX, NZ), F32),
            pltpu.VMEM((NX, NZ), F32),
            pltpu.VMEM((2, HALO, NY, NZ), F32),
            pltpu.SemaphoreType.DMA,
            pltpu.SemaphoreType.DMA((3,)),
            pltpu.SemaphoreType.DMA((2,)),
            pltpu.SemaphoreType.DMA((2,)),
            pltpu.SemaphoreType.DMA((2,)),
        ],
        compiler_params=pltpu.CompilerParams(vmem_limit_bytes=60 * 1024 * 1024),
        cost_estimate=pl.CostEstimate(flops=1000, bytes_accessed=2**20, transcendentals=0),
        name="depart",
    )(block, shift, recorded.reshape(NX, NZ), estimate)


def pick_taps(taps_ref, count, tap_index, valid):
    total = taps_ref[0, 0]
    picked = jnp.zeros(tap_index.shape, F32)
    for tap in range(count):
        if tap:
            total = total + taps_ref[0, tap]
        picked = jnp.where(tap_index == tap, taps_ref[0, tap], picked)
    if valid is not None:
        picked = jnp.where(valid, picked, 0.0)
    return picked / jnp.full(tap_index.shape, total, F32)


def packed(matrix, part):
    high, low = split(matrix)
    return jnp.where(part < 2, high.astype(F32), low.astype(F32)).astype(BF16)


def x_places(first, odd, turned):
    shape = (SLAB, 3 * WIDE)
    row, col = iota(shape, 0), iota(shape, 1)
    part = jnp.where(col >= 2 * WIDE, 2, jnp.where(col >= WIDE, 1, 0))
    col = col - part * WIDE
    block = lax.div(col, HALO)
    other = 4 - block if turned else jnp.where((block == 0) | (block == 4), 4 - block, block)
    block_at = jnp.where(odd == 1, other, block)
    return first + row, block_at * HALO + lax.rem(col, HALO) - HALO - row, part


def bands_kernel(group, block, shift_ref, x_ref, y_ref, z_ref, yf_ref, yb_ref, zf_ref, zb_ref, xf_ref, xb_ref):
    shift = shift_ref[0]
    first = block[0] * SLAB
    shape = (NY, 3 * NY)
    row, col = iota(shape, 0), iota(shape, 1)
    part = jnp.where(col >= 2 * NY, 2, jnp.where(col >= NY, 1, 0))
    col = col - part * NY
    yf_ref[...] = packed(pick_taps(y_ref, TAPS_Y, col - row + HALF_Y, None), part)
    row = lax.rem(row + group[0] * QUARTER, NY)
    yb_ref[...] = packed(pick_taps(y_ref, TAPS_Y, row - col + HALF_Y, None), part)
    shape = (NZ, NZ)
    row, col = iota(shape, 0), iota(shape, 1)
    for ref, index in ((zf_ref, row - col + HALF_Z), (zb_ref, col - row + HALF_Z)):
        high, low = split(pick_taps(z_ref, TAPS_Z, index, None))
        ref[:NZ, :NZ] = high
        ref[NZ:, :NZ] = high
        ref[:NZ, NZ:] = low
        ref[NZ:, NZ:] = jnp.zeros(shape, BF16)
    odd = lax.rem(block[0], 2)
    place, step, part = x_places(first, odd, False)
    view_row = place - shift
    view_row = jnp.where(view_row < 0, view_row + NX, view_row)
    view_row = jnp.where(view_row >= NX, view_row - NX, view_row)
    met = view_row + shift + step
    xf_ref[...] = packed(pick_taps(x_ref, TAPS_X, step + HALF_X, (met >= 0) & (met < NX)), part)
    place, step, part = x_places(first, odd, True)
    met = place - shift + step
    xb_ref[...] = packed(pick_taps(x_ref, TAPS_X, HALF_X - step, (met >= 0) & (met < NX)), part)


def make_bands(group, block, shift, psf_x, psf_y, psf_z):
    shapes = [(NY, 3 * NY)] * 2 + [(2 * NZ, 2 * NZ)] * 2 + [(SLAB, 3 * WIDE)] * 2
    return pl.pallas_call(
        bands_kernel,
        out_shape=[jax.ShapeDtypeStruct(shape, BF16) for shape in shapes],
        in_specs=[SMEM_SPEC] * 6,
        out_specs=[VMEM_SPEC] * 6,
        compiler_params=PARAMS,
        name="make_bands",
    )(group, block, shift, psf_x, psf_y, psf_z)


def blur_z(value, band):
    both = jnp.dot(jnp.concatenate(split(value), axis=1), band, preferred_element_type=F32)
    return both[:, :NZ] + both[:, NZ:]


def blur_rows(band, left, right):
    high, low = split(jnp.concatenate([left, right], axis=1))
    both = jnp.dot(band, jnp.concatenate([high, low, high], axis=0), preferred_element_type=F32)
    return both[:, :NZ], both[:, NZ:]


def forward_kernel(far_ref, own_ref, near_ref, yf_ref, zf_ref, xf_ref, out_ref, blurred, wide):
    for ref, count, base in ((far_ref, HALO, 0), (own_ref, SLAB, HALO), (near_ref, HALO, HALO + SLAB)):

        def along_z(block, carry, ref=ref, base=base):
            rows = ref[pl.ds(block * 8, 8)].reshape(8 * NY, NZ)
            start = pl.multiple_of((base + block * 8) * NY, 8)
            blurred[pl.ds(start, 8 * NY), :] = blur_z(rows, zf_ref[...])
            return carry

        lax.fori_loop(0, count // 8, along_z, 0)

    def along_y(pair, carry):
        start = pl.multiple_of(pair * 2 * NY, 2 * NY)
        left, right = blur_rows(yf_ref[...], blurred[pl.ds(start, NY), :], blurred[pl.ds(start + NY, NY), :])
        wide[pl.ds(start, NY), :] = left
        wide[pl.ds(start + NY, NY), :] = right
        return carry

    lax.fori_loop(0, WIDE // 2, along_y, 0, unroll=4)

    def along_x(pair, carry):
        y = pair * 2
        left, right = blur_rows(
            xf_ref[...], wide[pl.ds(y, WIDE, stride=NY), :], wide[pl.ds(y + 1, WIDE, stride=NY), :]
        )
        out_ref[y] = left
        out_ref[y + 1] = right
        return carry

    lax.fori_loop(0, NY // 2, along_x, 0, unroll=4)


def forward(far, own, near, band_y, band_z, band_x):
    return pl.pallas_call(
        forward_kernel,
        out_shape=jax.ShapeDtypeStruct((NY, SLAB, NZ), F32),
        in_specs=[VMEM_SPEC] * 6,
        out_specs=VMEM_SPEC,
        scratch_shapes=[pltpu.VMEM((WIDE * NY, NZ), F32), pltpu.VMEM((WIDE * NY, NZ), F32)],
        compiler_params=PARAMS,
        cost_estimate=pl.CostEstimate(flops=2 * 10**11, bytes_accessed=6 * 2**20, transcendentals=0),
        name="forward",
    )(far, own, near, band_y, band_z, band_x)


def quotient_kernel(block, scalars, seen_ref, predicted_ref, yb_ref, zb_ref, *rest):
    out_refs, (across_ref, rest_ref), (fetched, blurred, sems) = rest[:3], rest[3:5], rest[5:]
    odd = lax.rem(block[0], 2)
    size = NY // FETCHES
    copies = [
        pltpu.make_async_copy(
            seen_ref.at[pl.ds(part * size, size)], fetched.at[pl.ds(part * size, size)], sems.at[part]
        )
        for part in range(FETCHES)
    ]
    for copy in copies:
        copy.start()
    row = block[0] * SLAB - scalars[0] + iota((SLAB, NZ), 0)
    row = jnp.where(row < 0, row + NX, row)
    row = jnp.where(row >= NX, row - NX, row)
    inside = (row >= scalars[1]) & (row < scalars[2])
    for part in range(FETCHES):
        copies[part].wait()
        for y in range(part * size, (part + 1) * size, 16):
            span = pl.ds(y, 16)
            ratio = jnp.where(inside[None], fetched[span] / predicted_ref[span], 1.0)
            blurred[pl.ds(y * SLAB, 16 * SLAB), :] = blur_z(ratio.reshape(16 * SLAB, NZ), zb_ref[...])
    for index, first in enumerate((odd * (SLAB - HALO), (1 - odd) * (SLAB - HALO), HALO)):
        for x in range(0, HALO, 2):
            both = blur_rows(
                yb_ref[...],
                blurred[pl.ds(first + x, NY, stride=SLAB), :],
                blurred[pl.ds(first + x + 1, NY, stride=SLAB), :],
            )
            for side, plane in enumerate(both):
                out_refs[index][x + side] = plane
                if index == 0:
                    across_ref[x + side] = plane[2 * QUARTER : 3 * QUARTER]
                    rest_ref[x + side, : 2 * QUARTER] = plane[: 2 * QUARTER]
                    rest_ref[x + side, 2 * QUARTER :] = plane[3 * QUARTER :]


def quotient(block, scalars, seen, predicted, band_y, band_z):
    sizes = (NY, NY, NY, QUARTER, 3 * QUARTER)
    return pl.pallas_call(
        quotient_kernel,
        out_shape=[jax.ShapeDtypeStruct((HALO, size, NZ), F32) for size in sizes],
        in_specs=[SMEM_SPEC] * 2 + [ANY_SPEC] + [VMEM_SPEC] * 3,
        out_specs=[VMEM_SPEC] * len(sizes),
        scratch_shapes=[
            pltpu.VMEM((NY, SLAB, NZ), F32),
            pltpu.VMEM((NY * SLAB, NZ), F32),
            pltpu.SemaphoreType.DMA((FETCHES,)),
        ],
        compiler_params=PARAMS,
        cost_estimate=SHORT,
        name="quotient",
    )(block, scalars, seen, predicted, band_y, band_z)


def backward_kernel(parts, size, piece_ref, *rest):
    whole_refs, band_ref, out_refs = rest[:4], rest[4], rest[5:]
    for out_ref, (at, piece_at) in zip(out_refs, parts):
        for y in range(0, 8, 2):
            planes = [
                jnp.concatenate(
                    [piece_ref[pl.ds(piece_at + y + side, HALO, stride=size), :]]
                    + [ref[pl.ds(at + y + side, HALO, stride=NY), :] for ref in whole_refs],
                    axis=0,
                )
                for side in (0, 1)
            ]
            left, right = blur_rows(band_ref[...], *planes)
            out_ref[y] = left
            out_ref[y + 1] = right


def backward(parts, cost, piece, wholes, band_x):
    size = piece.shape[1]
    return pl.pallas_call(
        functools.partial(backward_kernel, parts, size),
        out_shape=[jax.ShapeDtypeStruct((8, SLAB, NZ), F32)] * len(parts),
        in_specs=[VMEM_SPEC] * 6,
        out_specs=[VMEM_SPEC] * len(parts),
        compiler_params=PARAMS,
        cost_estimate=cost,
        name="backward",
    )(piece.reshape(HALO * size, NZ), *[whole.reshape(HALO * NY, NZ) for whole in wholes], band_x)


def finish_rows(group, estimate_ref, piece_ref, turns, half, out_ref, out_base):
    base = pl.multiple_of(lax.rem(group[0] + turns, 4) * 16 + half * 8, 8)
    at = base if out_base is None else out_base

    def row(x, carry):
        value = piece_ref[pl.ds(x, 8, stride=SLAB), :]
        out_ref[x, pl.ds(at, 8), :] = estimate_ref[x, pl.ds(base, 8), :] * value * 0.25
        return carry

    lax.fori_loop(0, SLAB, row, 0, unroll=8)
    return base


def finish_kernel(parts, group, estimate_ref, *rest):
    piece_refs, out_ref = rest[:-1], rest[-1]
    for piece_ref, (turns, half) in zip(piece_refs, parts):
        finish_rows(group, estimate_ref, piece_ref, turns, half, out_ref, None)


def last_kernel(parts, group, estimate_ref, *rest):
    piece_refs, (_, out_ref, done, sems) = rest[: len(parts)], rest[len(parts) :]
    copies = []
    for index, (piece_ref, (turns, half)) in enumerate(zip(piece_refs, parts)):
        base = finish_rows(group, estimate_ref, piece_ref, turns, half, done, index * 8)
        copy = pltpu.make_async_copy(
            done.at[:, pl.ds(index * 8, 8), :], out_ref.at[:, pl.ds(base, 8), :], sems.at[index]
        )
        copy.start()
        copies.append(copy)
    for copy in copies:
        copy.wait()


def finish(parts, group, estimate, pieces, before=None):
    count = len(parts)
    pieces = [piece.reshape(8 * SLAB, NZ) for piece in pieces]
    shape = jax.ShapeDtypeStruct((SLAB, NY, NZ), F32)
    cost = SHORT
    in_specs = [SMEM_SPEC] + [VMEM_SPEC] * (count + 1)
    if before is None:
        return pl.pallas_call(
            functools.partial(finish_kernel, parts),
            out_shape=shape,
            in_specs=in_specs,
            out_specs=VMEM_SPEC,
            compiler_params=PARAMS,
            cost_estimate=cost,
            name="finish",
        )(group, estimate, *pieces)
    return pl.pallas_call(
        functools.partial(last_kernel, parts),
        out_shape=shape,
        in_specs=in_specs + [ANY_SPEC],
        out_specs=ANY_SPEC,
        scratch_shapes=[pltpu.VMEM((SLAB, 8 * count, NZ), F32), pltpu.SemaphoreType.DMA((count,))],
        input_output_aliases={count + 2: 0},
        compiler_params=PARAMS,
        cost_estimate=cost,
        name="finish_last",
    )(group, estimate, *pieces, before)


def turn(block, axis, step):
    size = lax.axis_size(axis)
    return lax.ppermute(block, axis, [(i, (i + step) % size) for i in range(size)])


def body(estimate, recorded, psf_x, psf_y, psf_z, view_shifts, view_boxes):
    group, block = lax.axis_index("group").reshape(1), lax.axis_index("block").reshape(1)
    rolled, far, near = depart(block, view_shifts, recorded, estimate)
    scalars = jnp.concatenate([view_shifts, view_boxes[0]])
    far, near = swap(far, True), swap(near, False)
    seen = lax.all_to_all(rolled.reshape(NY, SLAB, NZ), "block", 0, 0)
    yf, yb, zf, zb, xf, xb = make_bands(group, block, scalars, psf_x, psf_y, psf_z)
    predicted = forward(far, estimate, near, yf, zf, xf)

    far, near, middle, across, rest = quotient(block, scalars, seen, predicted, yb, zb)
    across, from_near, rest = swap(across, True), swap(near, False), swap(rest, True)
    wholes = (far, middle, near, from_near)

    far_a, far_b = backward(((32, 0), (40, 8)), FAR_COST, across, wholes, xb)
    far_a, far_b = turn(far_a, "group", 1), turn(far_b, "group", -1)
    next_a, near_b, near_a, prev_b, own_a, own_b = backward(
        ((16, 16), (24, 24), (48, 32), (56, 40), (0, 0), (8, 8)), SHORT, rest, wholes, xb
    )
    sum_a = turn(next_a + far_a, "group", 1)
    sum_b = turn(prev_b + far_b, "group", -1)
    near_b, near_a = turn(near_b, "group", 1), turn(near_a, "group", -1)
    near_b, near_a = lax.optimization_barrier((near_b, near_a))
    own_a = own_a + near_a + sum_a
    own_b = own_b + near_b + sum_b

    low_a, high_b = turn(own_a, "group", 1), turn(own_b, "group", -1)
    low_b, high_a = turn(own_b, "group", 1), turn(own_a, "group", -1)
    across_a, across_b = turn(low_a, "group", 1), turn(high_b, "group", -1)
    most = finish(
        ((0, 0), (0, 1), (3, 0), (3, 1), (1, 0), (1, 1)),
        group,
        estimate,
        (own_a, own_b, low_a, low_b, high_a, high_b),
    )
    most = finish(((2, 0),), group, estimate, (across_a,), most)
    return finish(((2, 1),), group, estimate, (across_b,), most)


def solution(mesh):
    return jax.shard_map(
        body,
        mesh=mesh,
        in_specs=(
            P("block", None, None),
            P("group", "block", None, None),
            P("group", None),
            P("group", None),
            P("group", None),
            P("group"),
            P("group", None),
        ),
        out_specs=P("block", None, None),
        check_vma=False,
    )
```
